32 devices in a mesh: expert: 16 (over z, y, x), dp: 2 (over core).
Axes of the slice: x: 2, y: 2, z: 4, core: 2. Of those that a mesh axis runs over, the one named last changes fastest.
Arguments:
- tokens: bfloat16 [1536, 4096], P('expert', 'dp'), may hold values from -6 to 6
- route_weight: float32 [1536, 8], P('expert'), may hold values from 0.05 to 0.25
- route_expert: int32 [1536, 8], P('expert'), may hold values from 0 to 15, all different within a row; in each aligned block of 96 rows (0 to 95, 96 to 191, ...) at most 64 rows name the same one
- cotangent: bfloat16 [1536, 4096], P('expert', 'dp'), may hold values from -6 to 6
- gate_quant: bfloat16 [16, 4096, 1024], P('expert', None, 'dp'), may hold values from -0.09375 to 0.09375
- up_quant: bfloat16 [16, 4096, 1024], P('expert', None, 'dp'), may hold values from -0.09375 to 0.09375
- gate_scale: float32 [16, 32, 8], P('expert', None, 'dp'), may hold values from 0.5 to 2
- up_scale: float32 [16, 32, 8], P('expert', None, 'dp'), may hold values from 0.5 to 2
- down_quant: bfloat16 [16, 1024, 4096], P('expert', None, 'dp'), may hold values from -0.1875 to 0.1875
- down_scale: float32 [16, 8, 32], P('expert', None, 'dp'), may hold values from 0.5 to 2
- first_moment: float32 [16, 1024, 4096], P('expert', None, 'dp'), may hold values from -6 to 6
- second_moment: float32 [16, 1024, 4096], P('expert', None, 'dp'), may hold values from 0.5 to 8
- old_expert: int32 [16], replicated, may hold values from 0 to 15, each once
- new_holder: int32 [16], replicated, may hold values from 0 to 15, each once
Outputs:
- mixed: bfloat16 [1536, 4096], P('expert', 'dp')
- new_down: bfloat16 [16, 1024, 4096], P('expert', None, 'dp')
- new_first: float32 [16, 1024, 4096], P('expert', None, 'dp')
- new_second: float32 [16, 1024, 4096], P('expert', None, 'dp')
The draws below stay inside these ranges and needn't reach their ends.
Inputs may be any that keep to these rules, and one draw needn't show every extreme that they name: `route_expert`: within each aligned block of 96 tokens (the tokens of one index of expert) no expert is named by more than 64 routes, a bound that some block reaches; a token names 8 different experts. `old_expert`: A permutation of the experts. `new_holder`: A permutation of the indices of expert.
All inputs are finite; a program needn't handle non-finite values.
Results may differ from the reference program's by a relative error of at most 0.0076.
Values may be sent and summed in bfloat16 or wider, within the bound.
No kernel may reach another device: no remote copies, remote signals or barrier semaphores. Data moves between devices by JAX's collectives and lax.ppermute only.
A program may use at most 256 MiB of HBM per device.

```python
import math
import jax
import jax.numpy as jnp
import numpy as np
from jax import lax

D = 4096
TOPK = 8
H = 1024
QB = 128
T_DEV = 96
EXPERTS = 16
TOKENS = 1536
CAP = 64


def block_scale(rng, extent, split, smallest, top_value):
    gain = 1.0
    for dim, blocks in split:
        draws = jax.random.uniform(jax.random.fold_in(jax.random.fold_in(rng, 6), dim), (blocks,), jnp.float32, smallest / len(split), top_value / len(split))
        gain = gain * jnp.repeat(jnp.exp(draws), extent[dim] // blocks).reshape((-1,) + (1,) * (len(extent) - 1 - dim))
    return gain


def shared_out(own_key, own, number, rows, number_of, top, limit, skew):
    order = jax.random.permutation(own_key, number_of)
    crowded, ordinary = load_shares(number_of, rows * top, limit, skew, True), load_shares(number_of, rows * top, limit, skew, False)
    places = jnp.arange(number_of)

    def named(sizes, offset_by):
        used = int((sizes > 0).sum())
        fixed = max(1, used // 4)
        passed = fixed + (places - fixed + offset_by * (used - fixed)) % max(1, number_of - fixed)
        return jnp.zeros((number_of,), jnp.int32).at[order[jnp.where(places < fixed, places, passed)]].set(jnp.asarray(sizes, jnp.int32))

    sizes = jnp.where(number % 4 == 0, named(crowded, number // 4), named(ordinary, number - number // 4 - 1))
    mixed = jax.random.permutation(jax.random.fold_in(own, 3), number_of)
    giver, sink = mixed[0:number_of // 2 * 2:2], mixed[1:number_of // 2 * 2:2]
    room = jnp.minimum(sizes[giver] - 1, limit - sizes[sink]) // 2
    room = jnp.where((giver == order[0]) | (sink == order[0]) | (sizes[sink] == 0), 0, jnp.maximum(room, 0))
    passed = jax.random.randint(jax.random.fold_in(own, 4), (number_of // 2,), 0, 1 << 20) % (room + 1)
    sizes = sizes.at[giver].add(-passed).at[sink].add(passed)
    members = jnp.searchsorted(jnp.cumsum(sizes), jnp.arange(rows * top), side="right").astype(jnp.int32)
    table = members.reshape(top, rows).T
    table = table[jax.random.permutation(jax.random.fold_in(own, 1), rows)]
    offset_by = jax.random.randint(jax.random.fold_in(own, 2), (rows, 1), 0, top)
    return jnp.take_along_axis(table, (jnp.arange(top)[None, :] + offset_by) % top, axis=1)


def load_shares(number_of, total, bound, slope, full):
    loads = [(1 << 20) // math.isqrt(rank ** slope) + 1 for rank in range(1, number_of + 1)]
    largest = bound if full else min(bound, max(-(-total // number_of), total * loads[0] // sum(loads)))
    least = 1 if total - largest >= number_of - 1 else 0
    counts, rest = [largest] + [least] * (number_of - 1), total - largest - least * (number_of - 1)
    while rest > 0:
        free = [i for i in range(1, number_of) if counts[i] < largest] or [i for i in range(1, number_of) if counts[i] < bound]
        pool, budget = sum([loads[i] for i in free]), rest
        for i in free:
            addition = min(bound - counts[i], max(1, budget * loads[i] // pool), rest)
            counts[i] = counts[i] + addition
            rest = rest - addition
    return np.array(counts)


def centred(stream_key, extent, spread, most, pieces=(), held_as=jnp.bfloat16):
    level = block_scale(stream_key, extent, pieces, -0.22, 0.18) if pieces else 1.0
    entries = jax.random.normal(stream_key, extent, jnp.float32) * spread * level
    return jnp.minimum(jnp.maximum(entries, -most), most).astype(held_as)


def setup_inputs(seed: int = 0) -> dict:
    keys = jax.random.split(jax.random.key(seed), 15)
    tokens = centred(keys[0], (TOKENS, D), 1.0, 6.0, ((0, 16), (1, 2)))
    route_weight = jnp.clip(0.05 + 0.2 * jax.random.uniform(keys[1], (TOKENS, TOPK), jnp.float32) ** block_scale(keys[1], (TOKENS, TOPK), ((0, 16),), -0.2, 0.2), 0.05, 0.25)
    route_expert_keys = jax.random.split(jax.random.fold_in(keys[2], 1), TOKENS // T_DEV)
    route_expert_turns = jax.random.permutation(jax.random.fold_in(keys[2], 3), TOKENS // T_DEV)
    route_expert = jax.vmap(lambda own, number: shared_out(jax.random.fold_in(keys[2], 2), own, number, T_DEV, EXPERTS, TOPK, CAP, 1))(route_expert_keys, route_expert_turns).reshape((TOKENS, TOPK))
    cotangent = centred(keys[3], (TOKENS, D), 1.0, 6.0, ((0, 16), (1, 2)))
    gate_quant = centred(keys[4], (EXPERTS, D, H), D ** -0.5, 0.09375, ((0, 16), (2, 2)))
    up_quant = centred(keys[5], (EXPERTS, D, H), D ** -0.5, 0.09375, ((0, 16), (2, 2)))
    gate_scale = jnp.clip(jnp.exp(math.log(2.0) - 1.3862944 * jax.random.uniform(keys[6], (EXPERTS, D // QB, H // QB), jnp.float32) ** block_scale(keys[6], (EXPERTS, D // QB, H // QB), ((0, 16), (2, 2)), -0.2, 0.2)), 0.5, 2.0)
    up_scale = jnp.clip(jnp.exp(math.log(2.0) - 1.3862944 * jax.random.uniform(keys[7], (EXPERTS, D // QB, H // QB), jnp.float32) ** block_scale(keys[7], (EXPERTS, D // QB, H // QB), ((0, 16), (2, 2)), -0.2, 0.2)), 0.5, 2.0)
    down_quant = centred(keys[8], (EXPERTS, H, D), H ** -0.5, 0.1875, ((0, 16), (2, 2)))
    down_scale = jnp.clip(jnp.exp(math.log(2.0) - 1.3862944 * jax.random.uniform(keys[9], (EXPERTS, H // QB, D // QB), jnp.float32) ** block_scale(keys[9], (EXPERTS, H // QB, D // QB), ((0, 16), (2, 2)), -0.2, 0.2)), 0.5, 2.0)
    first_moment = centred(keys[10], (EXPERTS, H, D), 1.0, 6.0, ((0, 16), (2, 2)), jnp.float32)
    second_moment = jnp.clip(jnp.exp(math.log(8.0) - 2.7725887 * jax.random.uniform(keys[11], (EXPERTS, H, D), jnp.float32) ** block_scale(keys[11], (EXPERTS, H, D), ((0, 16), (2, 2)), -0.2, 0.2)), 0.5, 8.0)
    old_expert = jax.random.permutation(keys[12], EXPERTS).astype(jnp.int32)
    new_holder = jax.random.permutation(keys[13], EXPERTS).astype(jnp.int32)
    return {"tokens": tokens, "route_weight": route_weight, "route_expert": route_expert, "cotangent": cotangent, "gate_quant": gate_quant, "up_quant": up_quant, "gate_scale": gate_scale, "up_scale": up_scale, "down_quant": down_quant, "down_scale": down_scale, "first_moment": first_moment, "second_moment": second_moment, "old_expert": old_expert, "new_holder": new_holder}


beta_first = 0.9
beta_second = 0.95
adam_eps = 1e-08
learn_rate = 0.003
decay_rate = 0.1
step_count = 20

def dequantize(quant, scale):
    tiled = jnp.repeat(jnp.repeat(scale, QB, axis=0), QB, axis=1)
    return quant.astype(jnp.float32) * tiled

def adam_step(master, grad, first, second):
    first_new = beta_first * first + (1.0 - beta_first) * grad
    second_new = beta_second * second + (1.0 - beta_second) * grad * grad
    fix_first = 1.0 - beta_first ** step_count
    fix_second = 1.0 - beta_second ** step_count
    update = first_new / fix_first / (jnp.sqrt(second_new / fix_second) + adam_eps)
    fresh = (master - learn_rate * (update + decay_rate * master)).astype(jnp.bfloat16)
    return (fresh, first_new, second_new)

def reference(tokens, route_weight, route_expert, cotangent, gate_quant, up_quant, gate_scale, up_scale, down_quant, down_scale, first_moment, second_moment, old_expert, new_holder):
    route_count = TOKENS * TOPK
    rows_most = TOKENS // T_DEV * CAP
    flat_expert = route_expert.reshape(-1)
    flat_weight = route_weight.reshape(-1)
    route_ids = jnp.arange(route_count, dtype=jnp.int32)

    def per_expert(total, index):
        expert_id = old_expert[index]
        hit_mask = (flat_expert == expert_id).astype(jnp.int32)
        order_pos = jnp.cumsum(hit_mask) - 1
        target_pos = jnp.where(hit_mask > 0, order_pos, rows_most).astype(jnp.int32)
        slot_route = jnp.full((rows_most,), route_count, jnp.int32).at[target_pos].set(route_ids, mode='drop')
        live_rows = slot_route < route_count
        safe_route = jnp.minimum(slot_route, route_count - 1)
        token_ids = safe_route // TOPK
        rows_in = jnp.where(live_rows[:, None], tokens[token_ids], jnp.zeros((), jnp.bfloat16))
        gate_w = dequantize(gate_quant[index], gate_scale[index]).astype(jnp.bfloat16)
        up_w = dequantize(up_quant[index], up_scale[index]).astype(jnp.bfloat16)
        master = dequantize(down_quant[index], down_scale[index])
        down_w = master.astype(jnp.bfloat16)
        gate_val = jnp.dot(rows_in, gate_w, preferred_element_type=jnp.float32)
        up_val = jnp.dot(rows_in, up_w, preferred_element_type=jnp.float32)
        hidden = (jax.nn.silu(gate_val) * up_val).astype(jnp.bfloat16)
        out_rows = jnp.dot(hidden, down_w, preferred_element_type=jnp.float32).astype(jnp.bfloat16)
        weight_rows = jnp.where(live_rows, flat_weight[safe_route], jnp.float32(0.0))
        total = total.at[token_ids].add(weight_rows[:, None] * out_rows.astype(jnp.float32))
        back_rows = (weight_rows[:, None] * cotangent[token_ids].astype(jnp.float32)).astype(jnp.bfloat16)
        grad = lax.dot_general(hidden, back_rows, (((0,), (0,)), ((), ())), preferred_element_type=jnp.float32)
        fresh, first_new, second_new = adam_step(master, grad, first_moment[index], second_moment[index])
        return (total, (fresh, first_new, second_new))
    start = jnp.zeros((TOKENS, D), jnp.float32)
    total, stacked = lax.scan(per_expert, start, jnp.arange(EXPERTS, dtype=jnp.int32))
    labels = jnp.arange(EXPERTS, dtype=jnp.int32)
    takes = (new_holder[:, None] == labels[None, :]).astype(jnp.int32)
    giver = lax.optimization_barrier(jnp.sum(takes * labels[:, None], axis=0)).astype(jnp.int32)
    fresh_all, first_all, second_all = stacked
    return (total.astype(jnp.bfloat16), fresh_all[giver], first_all[giver], second_all[giver])
```

```python
import jax
import jax.numpy as jnp
from jax import lax
from jax.experimental import pallas as pl
from jax.experimental.pallas import tpu as pltpu
from jax.sharding import PartitionSpec as P

QB = 128
INNER = 4

beta_first = 0.9
beta_second = 0.95
adam_eps = 1e-08
learn_rate = 0.003
decay_rate = 0.1
step_count = 20
fix_first = 1.0 - beta_first**step_count
fix_second = 1.0 - beta_second**step_count


def dequantize(quant, scale):
    rows, columns = quant.shape
    across = jnp.repeat(scale, QB, axis=1)
    tiles = quant.astype(jnp.float32).reshape(rows // QB, QB, columns) * across[:, None, :]
    return tiles.reshape(rows, columns)


def swap(value, bits):
    number = lax.axis_size("expert")
    return lax.ppermute(value, "expert", [(i, i ^ bits) for i in range(number)])


def swap_part(value, bits):
    number = lax.axis_size("dp")
    return lax.ppermute(value, "dp", [(i, i ^ bits) for i in range(number)])


def part_pieces(value):
    number = lax.axis_size("dp")
    part = lax.axis_index("dp")
    held = [value] + [swap_part(value, q) for q in range(1, number)]
    pieces = []
    for p in range(number):
        piece = held[0]
        for q in range(1, number):
            piece = jnp.where((part ^ p) == q, held[q], piece)
        pieces.append(piece)
    return pieces


def gather_small(block):
    lines = gather_lines(block)
    lines = jnp.stack([lines, swap(lines, 1)], axis=1)
    lines = jnp.stack([lines, swap(lines, 2)], axis=1)
    return lines.reshape((-1,) + block.shape)


def after(value, *earlier):
    return lax.optimization_barrier((value,) + earlier)[0]


def gather_lines(block):
    outer = lax.axis_size("expert") // INNER
    return jnp.stack([block] + [swap(block, INNER * k) for k in range(1, outer)])


def gather_blocks(lines):
    outer, rows, columns = lines.shape
    half = columns // 2
    left, right = lines[:, :, :half], lines[:, :, half:]
    left = jnp.stack([left, swap(left, 1)], axis=1)
    right = jnp.stack([right, swap(right, 2)], axis=1)
    left = jnp.stack([left, swap(left, 2)], axis=1)
    right = jnp.stack([right, swap(right, 1)], axis=2)
    return left.reshape(-1, half), right.reshape(-1, half)


def add(mine, other):
    return mine.astype(jnp.float32) + other.astype(jnp.float32)


def scatter_inner(parts):
    number, rows, columns = parts.shape
    half = columns // 2
    grid = parts.reshape(number // INNER, 2, 2, rows, columns)
    left, right = grid[..., :half], grid[..., half:]
    left = add(left[:, 0], swap(left[:, 1], 2)).astype(jnp.bfloat16)
    right = add(right[:, :, 0], swap(right[:, :, 1], 1)).astype(jnp.bfloat16)
    left = add(left[:, 0], swap(left[:, 1], 1)).astype(jnp.bfloat16)
    right = add(right[:, 0], swap(right[:, 1], 2)).astype(jnp.bfloat16)
    return jnp.concatenate([left, right], axis=-1)


def scatter_lines(lines):
    total = lines[0].astype(jnp.float32)
    for k in range(1, lines.shape[0]):
        total = total + swap(lines[k], INNER * k).astype(jnp.float32)
    return total.astype(jnp.bfloat16)


def half_exchange(value):
    number = lax.axis_size("expert")
    half = number // 2
    groups = [list(range(half)), list(range(half, number))]
    return lax.all_to_all(
        value, "expert", split_axis=0, concat_axis=0, tiled=True, axis_index_groups=groups
    )


def routing(new_holder, me):
    number = new_holder.shape[0]
    half = number // 2
    side = me // half
    labels = jnp.arange(number, dtype=jnp.int32)
    crosses = ((new_holder // half) != (labels // half)).astype(jnp.int32)
    same = (labels[:, None] // half) == (labels[None, :] // half)
    earlier = same & (labels[None, :] < labels[:, None])
    rank = jnp.sum(jnp.where(earlier, crosses[None, :], 0), axis=1)
    slots = jnp.arange(half, dtype=jnp.int32)
    mine = (labels // half) == side
    leaves = (rank[None, :] == slots[:, None]) & (crosses[None, :] > 0) & mine[None, :]
    send = jnp.sum(jnp.where(leaves, labels[None, :] % half, 0), axis=1)
    takes = new_holder[None, :] == (slots + side * half)[:, None]
    giver = jnp.sum(jnp.where(takes, labels[None, :], 0), axis=1)
    rank_of = jnp.sum(jnp.where(takes, rank[None, :], 0), axis=1)
    local = (giver // half) == side
    count = jnp.sum(crosses) // 2
    return send, local, giver % half, rank_of, count


def pick_items(value, index):
    return jnp.stack([lax.dynamic_index_in_dim(value, index[k], 0, keepdims=False) for k in range(index.shape[0])])


def cross_some(value, send, start, size):
    return swap(pick_items(value, send[start : start + size]), value.shape[0])


def cross_rest(value, send, count):
    half = value.shape[0]
    base = half // 2
    sizes = sorted({0, half // 8, half // 4, half // 2})

    def branch(extra):
        def run(held):
            if extra == 0:
                return jnp.zeros((half - base,) + held.shape[1:], held.dtype)
            came = cross_some(held, send, base, extra)
            if extra == half - base:
                return came
            rest = jnp.zeros((half - base - extra,) + held.shape[1:], held.dtype)
            return jnp.concatenate([came, rest])

        return run

    over = count - base
    which = sum((over > s).astype(jnp.int32) for s in sizes[:-1])
    return lax.switch(which, [branch(s) for s in sizes], value)


def chosen(table, i, held):
    value = held[0][0]
    for k in range(1, len(held)):
        value = jnp.where(table[0, i] == k, held[k][0], value)
    return value.astype(jnp.float32)


def first_body(table, *refs):
    *held, grad, out = refs
    old = chosen(table, pl.program_id(0), held)
    out[0] = (beta_first * old + (1.0 - beta_first) * grad[0]).astype(out.dtype)


def second_body(table, *refs):
    *held, grad, out = refs
    old = chosen(table, pl.program_id(0), held)
    g = grad[0]
    out[0] = (beta_second * old + (1.0 - beta_second) * g * g).astype(out.dtype)


def fresh_body(table, *refs):
    *held, first, second, out = refs
    master = chosen(table, pl.program_id(0), held)
    mean = first[0].astype(jnp.float32) / fix_first
    scale = jnp.sqrt(second[0].astype(jnp.float32) / fix_second) + adam_eps
    out[0] = (master - learn_rate * (mean / scale + decay_rate * master)).astype(out.dtype)


def per_item(body, table, held, extras):
    items, rows, columns = held[0].shape
    block = (1, rows, columns)

    def held_spec(k):
        return pl.BlockSpec(block, lambda i, t: (t[1 + k, i], 0, 0))

    specs = [held_spec(k) for k in range(len(held))]
    specs += [pl.BlockSpec(block, lambda i, t: (i, 0, 0)) for _ in extras]
    return pl.pallas_call(
        body,
        grid_spec=pltpu.PrefetchScalarGridSpec(
            num_scalar_prefetch=1,
            grid=(items,),
            in_specs=specs,
            out_specs=pl.BlockSpec(block, lambda i, t: (i, 0, 0)),
        ),
        out_shape=jax.ShapeDtypeStruct(held[0].shape, jnp.bfloat16),
        compiler_params=pltpu.CompilerParams(vmem_limit_bytes=32 * 1024 * 1024),
        cost_estimate=pl.CostEstimate(
            flops=10 * held[0].size, bytes_accessed=(6 + 4 * len(extras)) * held[0].size, transcendentals=0
        ),
    )(table, *held, *extras)


def per_device(
    tokens,
    route_weight,
    route_expert,
    cotangent,
    gate_quant,
    up_quant,
    gate_scale,
    up_scale,
    down_quant,
    down_scale,
    first_moment,
    second_moment,
    old_expert,
    new_holder,
):
    number = lax.axis_size("expert")
    dp_size = lax.axis_size("dp")
    me = lax.axis_index("expert")
    part = lax.axis_index("dp")
    half = number // 2
    tok_rows = tokens.shape[0]
    hidden_rows, columns = down_quant.shape[1:]
    unit_rows = hidden_rows // half
    item_shape = (half, unit_rows, columns)

    send, local, giver_slot, rank_of, count = routing(new_holder, me)
    base = half // 2
    quarter = base // 2
    place = jnp.where(local, 0, 1 + jnp.minimum(rank_of // quarter, 2))
    table = jnp.stack(
        [
            place,
            jnp.where(local, giver_slot, 0),
            jnp.where(place == 1, rank_of, 0),
            jnp.where(place == 2, rank_of - quarter, 0),
            jnp.where(place == 3, rank_of - base, 0),
        ]
    ).astype(jnp.int32)

    token_lines = gather_lines(tokens)
    first_out = half_exchange(first_moment[0].astype(jnp.bfloat16).reshape(item_shape))
    blocks = jnp.arange(number, dtype=jnp.int32)
    labels = jnp.arange(number, dtype=jnp.int32)
    named = (route_expert[:, :, None] == labels).astype(jnp.float32)
    weight_own = jnp.sum(named * route_weight[:, :, None], axis=1)
    weight_all = gather_small(weight_own)
    held_label = jnp.sum(jnp.where(labels == me, old_expert, 0))
    weight_rows = jnp.sum(jnp.where(labels == held_label, weight_all, 0.0), axis=2).reshape(-1, 1)

    token_parts = gather_blocks(after(token_lines, first_out, weight_rows))
    first_a = cross_some(after(first_out, token_lines), send, 0, quarter)

    gate_up = jnp.concatenate(
        [
            dequantize(gate_quant[0], gate_scale[0]).astype(jnp.bfloat16),
            dequantize(up_quant[0], up_scale[0]).astype(jnp.bfloat16),
        ],
        axis=1,
    )
    down_w = dequantize(down_quant[0], down_scale[0]).astype(jnp.bfloat16)
    width = tokens.shape[1]
    whole = after(jnp.concatenate(token_parts, axis=1), first_a)
    first_b = cross_some(after(first_out, first_a), send, quarter, quarter)
    pieces = [whole] + [swap_part(whole, q) for q in range(1, dp_size)]
    value = 0.0
    for q, piece in enumerate(pieces):
        weights = lax.dynamic_slice_in_dim(gate_up, (part ^ q) * width, width, 0)
        value = value + jnp.dot(piece, weights, preferred_element_type=jnp.float32)
    units = gate_quant.shape[2]
    gate_val, up_val = value[:, :units], value[:, units:]
    hidden = (jax.nn.silu(gate_val) * up_val * weight_rows).astype(jnp.bfloat16)
    hidden = jnp.concatenate(part_pieces(hidden), axis=1)

    second_out = half_exchange(
        after(second_moment[0], *token_parts).astype(jnp.bfloat16).reshape(item_shape)
    )

    share = number // dp_size
    mine = me ^ (part * share + jnp.arange(share, dtype=jnp.int32))
    sent = jnp.take(hidden.reshape(number, tok_rows, hidden_rows), mine, axis=0)
    sent = sent.reshape(share * tok_rows, half, unit_rows).transpose(1, 0, 2)
    hid_own = half_exchange(after(sent, second_out, first_b))
    back_lines = gather_lines(after(cotangent, first_b))
    hid_came = swap(after(hid_own, back_lines), half)
    hid_items = jnp.where(
        local[:, None, None],
        jnp.take(hid_own, giver_slot, axis=0),
        jnp.take(hid_came, giver_slot, axis=0),
    )
    hid_items = jnp.concatenate(part_pieces(hid_items), axis=1)

    back_parts = gather_blocks(after(back_lines, hid_own))
    down_out = half_exchange(after(down_w, *back_parts).reshape(item_shape))
    second_a = cross_some(after(second_out, hid_came), send, 0, quarter)
    second_b = cross_some(after(second_out, second_a), send, quarter, quarter)
    down_a = cross_some(after(down_out, second_b), send, 0, quarter)
    down_b = cross_some(after(down_out, down_a), send, quarter, quarter)
    first_held = (first_out, first_a, first_b, cross_rest(first_out, send, count))
    second_held = (second_out, second_a, second_b, cross_rest(second_out, send, count))
    down_held = (down_out, down_a, down_b, cross_rest(down_out, send, count))

    back = jnp.concatenate(back_parts, axis=-1).reshape(number, tok_rows, columns)
    back = jnp.take(back, me ^ blocks, axis=0).reshape(number * tok_rows, columns)
    grad = lax.dot_general(
        hid_items, back, (((1,), (0,)), ((), ())), preferred_element_type=jnp.float32
    )

    out_part = jnp.dot(hidden, down_w, preferred_element_type=jnp.float32).astype(jnp.bfloat16)
    out_part = after(out_part, down_out, second_a).reshape(number, tok_rows, columns)
    mixed_lines = scatter_inner(out_part)

    first_new = per_item(first_body, table, first_held, (grad,))
    second_new = per_item(second_body, table, second_held, (grad,))
    first_home = half_exchange(after(first_new, mixed_lines, second_b))
    second_home = half_exchange(after(second_new, first_home, down_a))
    mixed = scatter_lines(after(mixed_lines, down_b))
    fresh = per_item(fresh_body, table, down_held, (first_new, second_new))
    fresh_home = half_exchange(after(fresh, second_home))

    home = (1, hidden_rows, columns)
    return (
        mixed,
        fresh_home.reshape(home),
        first_home.reshape(home).astype(jnp.float32),
        second_home.reshape(home).astype(jnp.float32),
    )


def solution(mesh):
    in_specs = (
        P("expert", "dp"),
        P("expert", None),
        P("expert", None),
        P("expert", "dp"),
        P("expert", None, "dp"),
        P("expert", None, "dp"),
        P("expert", None, "dp"),
        P("expert", None, "dp"),
        P("expert", None, "dp"),
        P("expert", None, "dp"),
        P("expert", None, "dp"),
        P("expert", None, "dp"),
        P(),
        P(),
    )
    out_specs = (
        P("expert", "dp"),
        P("expert", None, "dp"),
        P("expert", None, "dp"),
        P("expert", None, "dp"),
    )
    return jax.shard_map(
        per_device, mesh=mesh, in_specs=in_specs, out_specs=out_specs, check_vma=False
    )
```

```python
import jax
import jax.numpy as jnp
from jax import lax
from jax.experimental import pallas as pl
from jax.experimental.pallas import tpu as pltpu
from jax.sharding import PartitionSpec as P

QB = 128
INNER = 4

beta_first = 0.9
beta_second = 0.95
adam_eps = 1e-08
learn_rate = 0.003
decay_rate = 0.1
step_count = 20
fix_first = 1.0 - beta_first**step_count
fix_second = 1.0 - beta_second**step_count


def dequantize(quant, scale):
    rows, columns = quant.shape
    across = jnp.repeat(scale, QB, axis=1)
    tiles = quant.astype(jnp.float32).reshape(rows // QB, QB, columns) * across[:, None, :]
    return tiles.reshape(rows, columns)


def swap(value, bits):
    number = lax.axis_size("expert")
    return lax.ppermute(value, "expert", [(i, i ^ bits) for i in range(number)])


def swap_part(value, bits):
    number = lax.axis_size("dp")
    return lax.ppermute(value, "dp", [(i, i ^ bits) for i in range(number)])


def in_order(held):
    part = lax.axis_index("dp")
    pieces = []
    for p in range(len(held)):
        piece = held[0]
        for q in range(1, len(held)):
            piece = jnp.where((part ^ p) == q, held[q], piece)
        pieces.append(piece)
    return pieces


def all_parts(value):
    return [value] + [swap_part(value, q) for q in range(1, lax.axis_size("dp"))]


def fence(*values):
    return lax.optimization_barrier(values)


def after(value, *earlier):
    zero = 0.0
    for array in earlier:
        zero = zero + array[(-1,) * array.ndim].astype(jnp.float32) * 0.0
    return value + zero.astype(value.dtype)


def swap_turn(value, step):
    number, parts = lax.axis_size("expert"), lax.axis_size("dp")
    pairs = []
    for i in range(number):
        for p in range(parts):
            bits = 1 if (p + step) % 2 == 0 else 2
            pairs.append((i * parts + p, (i ^ bits) * parts + p))
    return lax.ppermute(value, ("expert", "dp"), pairs)


def in_turn(even, odd):
    return jnp.where(lax.axis_index("dp") % 2 == 0, even, odd)


def gather_lines(block):
    outer = lax.axis_size("expert") // INNER
    return jnp.stack([block] + [swap(block, INNER * k) for k in range(1, outer)])


def gather_near(lines):
    return jnp.stack([lines, swap_turn(lines, 0)])


def gather_far(pair):
    far = swap_turn(pair, 1)
    full = jnp.stack([pair[0], in_turn(pair[1], far[0]), in_turn(far[0], pair[1]), far[1]], axis=1)
    return full.reshape((-1,) + pair.shape[3:])


def add(mine, other):
    return mine.astype(jnp.float32) + other.astype(jnp.float32)


def scatter_far(parts):
    number, rows, columns = parts.shape
    grid = parts.reshape(number // INNER, INNER, rows, columns)
    near, far = in_turn(grid[:, 1], grid[:, 2]), in_turn(grid[:, 2], grid[:, 1])
    came = swap_turn(jnp.stack([far, grid[:, 3]]), 1)
    return add(grid[:, 0], came[0]).astype(jnp.bfloat16), add(near, came[1]).astype(jnp.bfloat16)


def scatter_near(kept, near):
    return add(kept, swap_turn(near, 0)).astype(jnp.bfloat16)


def scatter_lines(lines):
    total = lines[0].astype(jnp.float32)
    for k in range(1, lines.shape[0]):
        total = total + swap(lines[k], INNER * k).astype(jnp.float32)
    return total.astype(jnp.bfloat16)


def half_exchange(value):
    number = lax.axis_size("expert")
    half = number // 2
    groups = [list(range(half)), list(range(half, number))]
    return lax.all_to_all(
        value, "expert", split_axis=0, concat_axis=0, tiled=True, axis_index_groups=groups
    )


def routing(new_holder, me):
    number = new_holder.shape[0]
    half = number // 2
    side = me // half
    labels = jnp.arange(number, dtype=jnp.int32)
    crosses = ((new_holder // half) != (labels // half)).astype(jnp.int32)
    same = (labels[:, None] // half) == (labels[None, :] // half)
    earlier = same & (labels[None, :] < labels[:, None])
    rank = jnp.sum(jnp.where(earlier, crosses[None, :], 0), axis=1)
    slots = jnp.arange(half, dtype=jnp.int32)
    mine = (labels // half) == side
    leaves = (rank[None, :] == slots[:, None]) & (crosses[None, :] > 0) & mine[None, :]
    send = jnp.sum(jnp.where(leaves, labels[None, :] % half, 0), axis=1)
    takes = new_holder[None, :] == (slots + side * half)[:, None]
    giver = jnp.sum(jnp.where(takes, labels[None, :], 0), axis=1)
    rank_of = jnp.sum(jnp.where(takes, rank[None, :], 0), axis=1)
    local = (giver // half) == side
    count = jnp.sum(crosses) // 2
    return send, local, giver % half, rank_of, count


def pick_items(value, index):
    return jnp.stack([lax.dynamic_index_in_dim(value, index[k], 0, keepdims=False) for k in range(index.shape[0])])


def cross_some(value, send, start, size):
    return swap(pick_items(value, send[start : start + size]), value.shape[0])


def cross_rest(value, send, count):
    half = value.shape[0]
    base = half // 2
    sizes = sorted({0, half // 8, half // 4, half // 2})

    def branch(extra):
        def run(held):
            if extra == 0:
                return jnp.zeros((half - base,) + held.shape[1:], held.dtype)
            came = cross_some(held, send, base, extra)
            if extra == half - base:
                return came
            rest = jnp.zeros((half - base - extra,) + held.shape[1:], held.dtype)
            return jnp.concatenate([came, rest])

        return run

    over = count - base
    which = sum((over > s).astype(jnp.int32) for s in sizes[:-1])
    return lax.switch(which, [branch(s) for s in sizes], value)


def chosen(table, i, held):
    value = held[0][0]
    for k in range(1, len(held)):
        value = jnp.where(table[0, i] == k, held[k][0], value)
    return value.astype(jnp.float32)


def first_body(table, *refs):
    *held, grad, out = refs
    old = chosen(table, pl.program_id(0), held)
    out[0] = (beta_first * old + (1.0 - beta_first) * grad[0]).astype(out.dtype)


def second_body(table, *refs):
    *held, grad, out = refs
    old = chosen(table, pl.program_id(0), held)
    g = grad[0]
    out[0] = (beta_second * old + (1.0 - beta_second) * g * g).astype(out.dtype)


def fresh_body(table, *refs):
    *held, first, second, out = refs
    master = chosen(table, pl.program_id(0), held)
    mean = first[0].astype(jnp.float32) / fix_first
    scale = jnp.sqrt(second[0].astype(jnp.float32) / fix_second) + adam_eps
    out[0] = (master - learn_rate * (mean / scale + decay_rate * master)).astype(out.dtype)


def per_item(body, table, held, extras):
    items, rows, columns = held[0].shape
    block = (1, rows, columns)

    def held_spec(k):
        return pl.BlockSpec(block, lambda i, t: (t[1 + k, i], 0, 0))

    specs = [held_spec(k) for k in range(len(held))]
    specs += [pl.BlockSpec(block, lambda i, t: (i, 0, 0)) for _ in extras]
    return pl.pallas_call(
        body,
        grid_spec=pltpu.PrefetchScalarGridSpec(
            num_scalar_prefetch=1,
            grid=(items,),
            in_specs=specs,
            out_specs=pl.BlockSpec(block, lambda i, t: (i, 0, 0)),
        ),
        out_shape=jax.ShapeDtypeStruct(held[0].shape, jnp.bfloat16),
        compiler_params=pltpu.CompilerParams(vmem_limit_bytes=32 * 1024 * 1024),
        cost_estimate=pl.CostEstimate(
            flops=10 * held[0].size, bytes_accessed=(6 + 4 * len(extras)) * held[0].size, transcendentals=0
        ),
    )(table, *held, *extras)


def per_device(
    tokens,
    route_weight,
    route_expert,
    cotangent,
    gate_quant,
    up_quant,
    gate_scale,
    up_scale,
    down_quant,
    down_scale,
    first_moment,
    second_moment,
    old_expert,
    new_holder,
):
    number = lax.axis_size("expert")
    dp_size = lax.axis_size("dp")
    me = lax.axis_index("expert")
    part = lax.axis_index("dp")
    half = number // 2
    tok_rows = tokens.shape[0]
    hidden_rows, columns = down_quant.shape[1:]
    unit_rows = hidden_rows // half
    item_shape = (half, unit_rows, columns)

    send, local, giver_slot, rank_of, count = routing(new_holder, me)
    base = half // 2
    one, two = base // 4, base // 2

    def table_of(sizes):
        starts = [sum(sizes[:k]) for k in range(len(sizes) + 1)]
        piece = sum((rank_of >= start).astype(jnp.int32) for start in starts)
        place = jnp.where(local, 0, piece)
        rows = [place, jnp.where(local, giver_slot, 0)]
        rows += [jnp.where(place == 1 + k, rank_of - start, 0) for k, start in enumerate(starts)]
        return jnp.stack(rows).astype(jnp.int32)

    share = tok_rows // dp_size
    blocks = jnp.arange(number, dtype=jnp.int32)
    labels = jnp.arange(number, dtype=jnp.int32)
    rows_of = tokens.reshape(dp_size, share, -1)
    token_own = [lax.dynamic_index_in_dim(rows_of, part, 0, keepdims=False)]
    for q in range(1, dp_size):
        token_own.append(swap_part(lax.dynamic_index_in_dim(rows_of, part ^ q, 0, keepdims=False), q))
    token_own = jnp.concatenate(in_order(token_own), axis=1)
    gates = all_parts(gate_quant[0])
    ups = all_parts(up_quant[0])
    gate_scales = all_parts(gate_scale[0])
    up_scales = all_parts(up_scale[0])
    first_moment = first_moment[0].astype(jnp.bfloat16).reshape(item_shape)
    token_own = after(token_own, gates[-1], ups[-1], gate_scales[-1], up_scales[-1])
    token_lines = gather_lines(token_own)

    def own_rows(value):
        return lax.dynamic_slice_in_dim(value, part * share, share, 0)

    named = (own_rows(route_expert)[:, :, None] == labels).astype(jnp.float32)
    weight_own = jnp.sum(named * own_rows(route_weight)[:, :, None], axis=1)
    weight_lines = gather_lines(weight_own)
    back_lines = gather_lines(cotangent)
    first_out = half_exchange(first_moment)
    second_moment = second_moment[0].astype(jnp.bfloat16).reshape(item_shape)
    down_w = dequantize(down_quant[0], down_scale[0]).astype(jnp.bfloat16)
    columns_of = [gate for gate in zip(gates, gate_scales)] + [up for up in zip(ups, up_scales)]
    gate_up = jnp.concatenate(
        [dequantize(quant, scale).astype(jnp.bfloat16) for quant, scale in columns_of], axis=1
    )
    token_lines, weight_lines, back_lines, first_out, second_moment, down_w, gate_up = fence(
        token_lines, weight_lines, back_lines, first_out, second_moment, down_w, gate_up
    )

    token_pair = gather_near(after(token_lines, gate_up))
    weight_pair = gather_near(weight_lines)
    first_a = cross_some(first_out, send, 0, one)
    token_pair, weight_pair, first_a, first_out = fence(token_pair, weight_pair, first_a, first_out)

    whole = gather_far(token_pair)
    weight_all = gather_far(weight_pair)
    first_b = cross_some(first_out, send, one, one)
    whole, weight_all, first_b, first_out, second_moment = fence(
        whole, weight_all, first_b, first_out, second_moment
    )

    value = jnp.dot(whole, gate_up, preferred_element_type=jnp.float32)
    held_label = jnp.sum(jnp.where(labels == me, old_expert, 0))
    weight_rows = jnp.sum(jnp.where(labels == held_label, weight_all, 0.0), axis=1, keepdims=True)
    units = gate_quant.shape[2]
    hidden = []
    for q in range(dp_size):
        gate_val = value[:, q * units : (q + 1) * units]
        up_val = value[:, hidden_rows + q * units : hidden_rows + (q + 1) * units]
        hidden.append((jax.nn.silu(gate_val) * up_val * weight_rows).astype(jnp.bfloat16))
    hidden = jnp.concatenate(in_order(hidden), axis=1)
    sent = jnp.take(hidden.reshape(number, share, hidden_rows), me ^ blocks, axis=0)
    sent = sent.reshape(number * share, half, unit_rows).transpose(1, 0, 2)
    second_out = half_exchange(second_moment)
    first_c = cross_some(first_out, send, 2 * one, one)
    hidden, sent, second_out, first_c, first_out, back_lines = fence(
        hidden, sent, second_out, first_c, first_out, back_lines
    )

    hid_own = half_exchange(sent)
    back_pair = gather_near(back_lines)
    first_d = cross_some(first_out, send, 3 * one, one)
    hid_own, back_pair, first_d, first_out, hidden, second_out = fence(
        hid_own, back_pair, first_d, first_out, hidden, second_out
    )

    hid_came = cross_some(hid_own, send, 0, base)
    hid_rest = cross_rest(hid_own, send, count)
    back = gather_far(back_pair)
    hidden_all = in_order(all_parts(hidden.reshape(number, share, hidden_rows)))
    hidden_all = jnp.stack(hidden_all, axis=1).reshape(number * tok_rows, hidden_rows)
    hid_came, hid_rest, back, hidden_all, second_out, down_w = fence(
        hid_came, hid_rest, back, hidden_all, second_out, down_w
    )

    down_out = half_exchange(down_w.reshape(item_shape))
    second_a = cross_some(second_out, send, 0, two)
    hid_items = jnp.where(
        local[:, None, None],
        jnp.take(hid_own, giver_slot, axis=0),
        jnp.take(jnp.concatenate([hid_came, hid_rest]), rank_of, axis=0),
    )
    out_part = jnp.dot(after(hidden_all, second_a), down_w, preferred_element_type=jnp.float32).astype(jnp.bfloat16)
    back = back.reshape(number, dp_size, share, columns)
    backs = [jnp.take(back[:, p], me ^ blocks, axis=0).reshape(-1, columns) for p in range(dp_size)]
    down_out, second_a, hid_items, out_part, second_out, *backs = fence(
        down_out, second_a, hid_items, out_part, second_out, *backs
    )

    hid_parts = in_order(all_parts(hid_items))
    kept, near = scatter_far(out_part.reshape(number, tok_rows, columns))
    second_b = cross_some(second_out, send, two, two)
    grad = lax.dot_general(
        jnp.concatenate(hid_parts, axis=1),
        jnp.concatenate(backs, axis=0),
        (((1,), (0,)), ((), ())),
        preferred_element_type=jnp.float32,
    )
    first_held = (first_out, first_a, first_b, first_c, first_d, cross_rest(first_out, send, count))
    first_new = per_item(first_body, table_of((one, one, one, one)), first_held, (grad,))
    kept, near, second_b, grad, first_new, down_out = fence(
        kept, near, second_b, grad, first_new, down_out
    )

    first_home = half_exchange(first_new)
    down_a = cross_some(down_out, send, 0, two)
    lines = scatter_near(kept, near)
    second_held = (second_out, second_a, second_b, cross_rest(second_out, send, count))
    second_new = per_item(second_body, table_of((two, two)), second_held, (grad,))
    first_home, down_a, lines, second_new, down_out = fence(
        first_home, down_a, lines, second_new, down_out
    )

    second_home = half_exchange(second_new)
    down_b = cross_some(down_out, send, two, two)
    mixed = scatter_lines(lines)
    first_full = first_home.astype(jnp.float32)
    second_home, down_b, first_full, mixed = fence(second_home, down_b, first_full, mixed)

    down_held = (down_out, down_a, down_b, cross_rest(down_out, send, count))
    fresh = per_item(fresh_body, table_of((two, two)), down_held, (first_new, second_new))
    fresh_home = half_exchange(fresh)
    second_full = second_home.astype(jnp.float32)

    home = (1, hidden_rows, columns)
    return (mixed, fresh_home.reshape(home), first_full.reshape(home), second_full.reshape(home))


def solution(mesh):
    in_specs = (
        P("expert", "dp"),
        P("expert", None),
        P("expert", None),
        P("expert", "dp"),
        P("expert", None, "dp"),
        P("expert", None, "dp"),
        P("expert", None, "dp"),
        P("expert", None, "dp"),
        P("expert", None, "dp"),
        P("expert", None, "dp"),
        P("expert", None, "dp"),
        P("expert", None, "dp"),
        P(),
        P(),
    )
    out_specs = (
        P("expert", "dp"),
        P("expert", None, "dp"),
        P("expert", None, "dp"),
        P("expert", None, "dp"),
    )
    return jax.shard_map(
        per_device, mesh=mesh, in_specs=in_specs, out_specs=out_specs, check_vma=False
    )
```

```python
import jax
import jax.numpy as jnp
from jax import lax
from jax.experimental import pallas as pl
from jax.experimental.pallas import tpu as pltpu
from jax.sharding import PartitionSpec as P

QB = 128
INNER = 4

beta_first = 0.9
beta_second = 0.95
adam_eps = 1e-08
learn_rate = 0.003
decay_rate = 0.1
step_count = 20
fix_first = 1.0 - beta_first**step_count
fix_second = 1.0 - beta_second**step_count


def dequantize(quant, scale):
    rows, columns = quant.shape
    across = jnp.repeat(scale, QB, axis=1)
    tiles = quant.astype(jnp.float32).reshape(rows // QB, QB, columns) * across[:, None, :]
    return tiles.reshape(rows, columns)


def swap(value, bits):
    number = lax.axis_size("expert")
    return lax.ppermute(value, "expert", [(i, i ^ bits) for i in range(number)])


def swap_part(value, bits):
    number = lax.axis_size("dp")
    return lax.ppermute(value, "dp", [(i, i ^ bits) for i in range(number)])


def in_order(held):
    part = lax.axis_index("dp")
    pieces = []
    for p in range(len(held)):
        piece = held[0]
        for q in range(1, len(held)):
            piece = jnp.where((part ^ p) == q, held[q], piece)
        pieces.append(piece)
    return pieces


def all_parts(value):
    return [value] + [swap_part(value, q) for q in range(1, lax.axis_size("dp"))]


def after(value, *earlier):
    zero = 0.0
    for array in earlier:
        zero = zero + array[(-1,) * array.ndim].astype(jnp.float32) * 0.0
    return value + zero.astype(value.dtype)


def swap_turn(value, step):
    number, parts = lax.axis_size("expert"), lax.axis_size("dp")
    pairs = []
    for i in range(number):
        for p in range(parts):
            bits = 1 if (p + step) % 2 == 0 else 2
            pairs.append((i * parts + p, (i ^ bits) * parts + p))
    return lax.ppermute(value, ("expert", "dp"), pairs)


def in_turn(even, odd):
    return jnp.where(lax.axis_index("dp") % 2 == 0, even, odd)


def gather_lines(block):
    outer = lax.axis_size("expert") // INNER
    return jnp.stack([block] + [swap(block, INNER * k) for k in range(1, outer)])


def gather_near(lines):
    return jnp.stack([lines, swap_turn(lines, 0)])


def gather_far(pair):
    far = swap_turn(pair, 1)
    full = jnp.stack([pair[0], in_turn(pair[1], far[0]), in_turn(far[0], pair[1]), far[1]], axis=1)
    return full.reshape((-1,) + pair.shape[3:])


def add(mine, other):
    return mine.astype(jnp.float32) + other.astype(jnp.float32)


def scatter_far(parts):
    number, rows, columns = parts.shape
    grid = parts.reshape(number // INNER, INNER, rows, columns)
    near, far = in_turn(grid[:, 1], grid[:, 2]), in_turn(grid[:, 2], grid[:, 1])
    came = swap_turn(jnp.stack([far, grid[:, 3]]), 1)
    return add(grid[:, 0], came[0]).astype(jnp.bfloat16), add(near, came[1]).astype(jnp.bfloat16)


def scatter_near(kept, near):
    return add(kept, swap_turn(near, 0)).astype(jnp.bfloat16)


def scatter_lines(lines):
    total = lines[0].astype(jnp.float32)
    for k in range(1, lines.shape[0]):
        total = total + swap(lines[k], INNER * k).astype(jnp.float32)
    return total.astype(jnp.bfloat16)


def half_exchange(value):
    number = lax.axis_size("expert")
    half = number // 2
    groups = [list(range(half)), list(range(half, number))]
    return lax.all_to_all(
        value, "expert", split_axis=0, concat_axis=0, tiled=True, axis_index_groups=groups
    )


def routing(new_holder, me):
    number = new_holder.shape[0]
    half = number // 2
    side = me // half
    labels = jnp.arange(number, dtype=jnp.int32)
    crosses = ((new_holder // half) != (labels // half)).astype(jnp.int32)
    same = (labels[:, None] // half) == (labels[None, :] // half)
    earlier = same & (labels[None, :] < labels[:, None])
    rank = jnp.sum(jnp.where(earlier, crosses[None, :], 0), axis=1)
    slots = jnp.arange(half, dtype=jnp.int32)
    mine = (labels // half) == side
    leaves = (rank[None, :] == slots[:, None]) & (crosses[None, :] > 0) & mine[None, :]
    send = jnp.sum(jnp.where(leaves, labels[None, :] % half, 0), axis=1)
    takes = new_holder[None, :] == (slots + side * half)[:, None]
    giver = jnp.sum(jnp.where(takes, labels[None, :], 0), axis=1)
    rank_of = jnp.sum(jnp.where(takes, rank[None, :], 0), axis=1)
    local = (giver // half) == side
    count = jnp.sum(crosses) // 2
    return send, local, giver % half, rank_of, count


def pick_items(value, index):
    return jnp.stack([lax.dynamic_index_in_dim(value, index[k], 0, keepdims=False) for k in range(index.shape[0])])


def cross_some(value, send, start, size):
    return swap(pick_items(value, send[start : start + size]), value.shape[0])


def cross_rest(value, send, count):
    half = value.shape[0]
    base = half // 2
    sizes = sorted({0, half // 8, half // 4, half // 2})

    def branch(extra):
        def run(held):
            if extra == 0:
                return jnp.zeros((half - base,) + held.shape[1:], held.dtype)
            came = cross_some(held, send, base, extra)
            if extra == half - base:
                return came
            rest = jnp.zeros((half - base - extra,) + held.shape[1:], held.dtype)
            return jnp.concatenate([came, rest])

        return run

    over = count - base
    which = sum((over > s).astype(jnp.int32) for s in sizes[:-1])
    return lax.switch(which, [branch(s) for s in sizes], value)


def chosen(table, i, held):
    value = held[0][0]
    for k in range(1, len(held)):
        value = jnp.where(table[0, i] == k, held[k][0], value)
    return value.astype(jnp.float32)


def first_body(table, *refs):
    *held, grad, out = refs
    old = chosen(table, pl.program_id(0), held)
    out[0] = (beta_first * old + (1.0 - beta_first) * grad[0]).astype(out.dtype)


def second_body(table, *refs):
    *held, grad, out = refs
    old = chosen(table, pl.program_id(0), held)
    g = grad[0]
    out[0] = (beta_second * old + (1.0 - beta_second) * g * g).astype(out.dtype)


def fresh_body(table, *refs):
    *held, first, second, out = refs
    master = chosen(table, pl.program_id(0), held)
    mean = first[0].astype(jnp.float32) / fix_first
    scale = jnp.sqrt(second[0].astype(jnp.float32) / fix_second) + adam_eps
    out[0] = (master - learn_rate * (mean / scale + decay_rate * master)).astype(out.dtype)


def per_item(body, table, held, extras):
    items, rows, columns = held[0].shape
    block = (1, rows, columns)

    def held_spec(k):
        return pl.BlockSpec(block, lambda i, t: (t[1 + k, i], 0, 0))

    specs = [held_spec(k) for k in range(len(held))]
    specs += [pl.BlockSpec(block, lambda i, t: (i, 0, 0)) for _ in extras]
    return pl.pallas_call(
        body,
        grid_spec=pltpu.PrefetchScalarGridSpec(
            num_scalar_prefetch=1,
            grid=(items,),
            in_specs=specs,
            out_specs=pl.BlockSpec(block, lambda i, t: (i, 0, 0)),
        ),
        out_shape=jax.ShapeDtypeStruct(held[0].shape, jnp.bfloat16),
        compiler_params=pltpu.CompilerParams(vmem_limit_bytes=32 * 1024 * 1024),
        cost_estimate=pl.CostEstimate(
            flops=10 * held[0].size, bytes_accessed=(6 + 4 * len(extras)) * held[0].size, transcendentals=0
        ),
    )(table, *held, *extras)


def per_device(
    tokens,
    route_weight,
    route_expert,
    cotangent,
    gate_quant,
    up_quant,
    gate_scale,
    up_scale,
    down_quant,
    down_scale,
    first_moment,
    second_moment,
    old_expert,
    new_holder,
):
    number = lax.axis_size("expert")
    dp_size = lax.axis_size("dp")
    me = lax.axis_index("expert")
    part = lax.axis_index("dp")
    half = number // 2
    tok_rows = tokens.shape[0]
    hidden_rows, columns = down_quant.shape[1:]
    unit_rows = hidden_rows // half
    item_shape = (half, unit_rows, columns)

    send, local, giver_slot, rank_of, count = routing(new_holder, me)
    base = half // 2

    def table_of(sizes):
        starts = [sum(sizes[:k]) for k in range(len(sizes) + 1)]
        piece = sum((rank_of >= start).astype(jnp.int32) for start in starts)
        place = jnp.where(local, 0, piece)
        rows = [place, jnp.where(local, giver_slot, 0)]
        rows += [jnp.where(place == 1 + k, rank_of - start, 0) for k, start in enumerate(starts)]
        return jnp.stack(rows).astype(jnp.int32)

    share = tok_rows // dp_size
    blocks = jnp.arange(number, dtype=jnp.int32)
    labels = jnp.arange(number, dtype=jnp.int32)
    rows_of = tokens.reshape(dp_size, share, -1)
    token_own = [lax.dynamic_index_in_dim(rows_of, part, 0, keepdims=False)]
    for q in range(1, dp_size):
        token_own.append(swap_part(lax.dynamic_index_in_dim(rows_of, part ^ q, 0, keepdims=False), q))
    token_own = jnp.concatenate(in_order(token_own), axis=1)
    columns_of = list(zip(all_parts(gate_quant[0]), all_parts(gate_scale[0])))
    columns_of += list(zip(all_parts(up_quant[0]), all_parts(up_scale[0])))
    gate_up = jnp.concatenate(
        [dequantize(quant, scale).astype(jnp.bfloat16) for quant, scale in columns_of], axis=1
    )

    token_lines = gather_lines(token_own)

    def own_rows(value):
        return lax.dynamic_slice_in_dim(value, part * share, share, 0)

    named = (own_rows(route_expert)[:, :, None] == labels).astype(jnp.float32)
    weight_own = jnp.sum(named * own_rows(route_weight)[:, :, None], axis=1)
    weight_all = gather_far(gather_near(gather_lines(weight_own)))
    held_label = jnp.sum(jnp.where(labels == me, old_expert, 0))
    weight_rows = jnp.sum(jnp.where(labels == held_label, weight_all, 0.0), axis=1, keepdims=True)
    back_lines = gather_lines(cotangent)
    whole = gather_far(gather_near(after(token_lines, gate_up, weight_rows)))

    value = jnp.dot(whole, gate_up, preferred_element_type=jnp.float32)
    units = gate_quant.shape[2]
    hidden = []
    for q in range(dp_size):
        gate_val = value[:, q * units : (q + 1) * units]
        up_val = value[:, hidden_rows + q * units : hidden_rows + (q + 1) * units]
        hidden.append((jax.nn.silu(gate_val) * up_val * weight_rows).astype(jnp.bfloat16))
    hidden = jnp.concatenate(in_order(hidden), axis=1)

    first_moment = after(first_moment[0], whole, back_lines).astype(jnp.bfloat16)
    first_out = half_exchange(first_moment.reshape(item_shape))
    sent = jnp.take(after(hidden, first_out).reshape(number, share, hidden_rows), me ^ blocks, axis=0)
    hid_own = half_exchange(sent.reshape(number * share, half, unit_rows).transpose(1, 0, 2))
    second_moment = after(second_moment[0], hid_own).astype(jnp.bfloat16)
    second_out = half_exchange(second_moment.reshape(item_shape))
    down_w = dequantize(down_quant[0], down_scale[0]).astype(jnp.bfloat16)
    down_out = half_exchange(after(down_w, second_out).reshape(item_shape))

    hid_came = cross_some(hid_own, send, 0, base)
    first_came = cross_some(first_out, send, 0, base)
    second_came = cross_some(second_out, after(send, first_came), 0, base)
    down_came = cross_some(down_out, after(send, second_came), 0, base)
    first_held = (first_out, first_came, cross_rest(first_out, send, count))
    second_held = (second_out, second_came, cross_rest(second_out, send, count))
    down_held = (down_out, down_came, cross_rest(down_out, send, count))
    hid_rest = cross_rest(hid_own, send, count)

    hidden_all = in_order(all_parts(hidden.reshape(number, share, hidden_rows)))
    hidden_all = jnp.stack(hidden_all, axis=1).reshape(number * tok_rows, hidden_rows)
    out_part = jnp.dot(hidden_all, down_w, preferred_element_type=jnp.float32).astype(jnp.bfloat16)
    lines = scatter_near(*scatter_far(out_part.reshape(number, tok_rows, columns)))
    mixed = scatter_lines(lines)

    hid_items = jnp.where(
        local[:, None, None],
        jnp.take(hid_own, giver_slot, axis=0),
        jnp.take(jnp.concatenate([hid_came, hid_rest]), rank_of, axis=0),
    )
    back = gather_far(gather_near(after(back_lines, first_came)))
    back = back.reshape(number, dp_size, share, columns)
    backs = [jnp.take(back[:, p], me ^ blocks, axis=0).reshape(-1, columns) for p in range(dp_size)]
    grad = lax.dot_general(
        jnp.concatenate(in_order(all_parts(hid_items)), axis=1),
        jnp.concatenate(backs, axis=0),
        (((1,), (0,)), ((), ())),
        preferred_element_type=jnp.float32,
    )

    table = table_of((base,))
    first_new = per_item(first_body, after(table, second_came, lines), first_held, (grad,))
    first_home = half_exchange(first_new)
    second_new = per_item(second_body, after(table, down_came), second_held, (grad,))
    second_home = half_exchange(second_new)
    fresh = per_item(fresh_body, table, down_held, (first_new, second_new))
    fresh_home = half_exchange(fresh)

    home = (1, hidden_rows, columns)
    return (
        mixed,
        fresh_home.reshape(home),
        first_home.astype(jnp.float32).reshape(home),
        second_home.astype(jnp.float32).reshape(home),
    )


def solution(mesh):
    in_specs = (
        P("expert", "dp"),
        P("expert", None),
        P("expert", None),
        P("expert", "dp"),
        P("expert", None, "dp"),
        P("expert", None, "dp"),
        P("expert", None, "dp"),
        P("expert", None, "dp"),
        P("expert", None, "dp"),
        P("expert", None, "dp"),
        P("expert", None, "dp"),
        P("expert", None, "dp"),
        P(),
        P(),
    )
    out_specs = (
        P("expert", "dp"),
        P("expert", None, "dp"),
        P("expert", None, "dp"),
        P("expert", None, "dp"),
    )
    return jax.shard_map(
        per_device, mesh=mesh, in_specs=in_specs, out_specs=out_specs, check_vma=False
    )
```

```python
import jax
import jax.numpy as jnp
from jax import lax
from jax.experimental import pallas as pl
from jax.experimental.pallas import tpu as pltpu
from jax.sharding import PartitionSpec as P

QB = 128
INNER = 4

beta_first = 0.9
beta_second = 0.95
adam_eps = 1e-08
learn_rate = 0.003
decay_rate = 0.1
step_count = 20
fix_first = 1.0 - beta_first**step_count
fix_second = 1.0 - beta_second**step_count


def dequantize(quant, scale):
    rows, columns = quant.shape
    across = jnp.repeat(scale, QB, axis=1)
    tiles = quant.astype(jnp.float32).reshape(rows // QB, QB, columns) * across[:, None, :]
    return tiles.reshape(rows, columns)


def swap(value, bits):
    number = lax.axis_size("expert")
    return lax.ppermute(value, "expert", [(i, i ^ bits) for i in range(number)])


def swap_part(value, bits):
    number = lax.axis_size("dp")
    return lax.ppermute(value, "dp", [(i, i ^ bits) for i in range(number)])


def in_order(held):
    part = lax.axis_index("dp")
    pieces = []
    for p in range(len(held)):
        piece = held[0]
        for q in range(1, len(held)):
            piece = jnp.where((part ^ p) == q, held[q], piece)
        pieces.append(piece)
    return pieces


def all_parts(value):
    return [value] + [swap_part(value, q) for q in range(1, lax.axis_size("dp"))]


def fence(*values):
    return lax.optimization_barrier(values)


def after(value, *earlier):
    zero = 0.0
    for array in earlier:
        zero = zero + array[(-1,) * array.ndim].astype(jnp.float32) * 0.0
    return value + zero.astype(value.dtype)


def swap_turn(value, step):
    number, parts = lax.axis_size("expert"), lax.axis_size("dp")
    pairs = []
    for i in range(number):
        for p in range(parts):
            bits = 1 if (p + step) % 2 == 0 else 2
            pairs.append((i * parts + p, (i ^ bits) * parts + p))
    return lax.ppermute(value, ("expert", "dp"), pairs)


def in_turn(even, odd):
    return jnp.where(lax.axis_index("dp") % 2 == 0, even, odd)


def gather_lines(block):
    outer = lax.axis_size("expert") // INNER
    return jnp.stack([block] + [swap(block, INNER * k) for k in range(1, outer)])


def gather_near(lines):
    return jnp.stack([lines, swap_turn(lines, 0)])


def gather_far(pair):
    far = swap_turn(pair, 1)
    full = jnp.stack([pair[0], in_turn(pair[1], far[0]), in_turn(far[0], pair[1]), far[1]], axis=1)
    return full.reshape((-1,) + pair.shape[3:])


def add(mine, other):
    return mine.astype(jnp.float32) + other.astype(jnp.float32)


def scatter_far(parts):
    number, rows, columns = parts.shape
    grid = parts.reshape(number // INNER, INNER, rows, columns)
    near, far = in_turn(grid[:, 1], grid[:, 2]), in_turn(grid[:, 2], grid[:, 1])
    came = swap_turn(jnp.stack([far, grid[:, 3]]), 1)
    return add(grid[:, 0], came[0]).astype(jnp.bfloat16), add(near, came[1]).astype(jnp.bfloat16)


def scatter_near(kept, near):
    return add(kept, swap_turn(near, 0)).astype(jnp.bfloat16)


def scatter_lines(lines):
    total = lines[0].astype(jnp.float32)
    for k in range(1, lines.shape[0]):
        total = total + swap(lines[k], INNER * k).astype(jnp.float32)
    return total.astype(jnp.bfloat16)


def half_exchange(value):
    number = lax.axis_size("expert")
    half = number // 2
    groups = [list(range(half)), list(range(half, number))]
    return lax.all_to_all(
        value, "expert", split_axis=0, concat_axis=0, tiled=True, axis_index_groups=groups
    )


def routing(new_holder, me):
    number = new_holder.shape[0]
    half = number // 2
    side = me // half
    labels = jnp.arange(number, dtype=jnp.int32)
    crosses = ((new_holder // half) != (labels // half)).astype(jnp.int32)
    same = (labels[:, None] // half) == (labels[None, :] // half)
    earlier = same & (labels[None, :] < labels[:, None])
    rank = jnp.sum(jnp.where(earlier, crosses[None, :], 0), axis=1)
    slots = jnp.arange(half, dtype=jnp.int32)
    mine = (labels // half) == side
    leaves = (rank[None, :] == slots[:, None]) & (crosses[None, :] > 0) & mine[None, :]
    send = jnp.sum(jnp.where(leaves, labels[None, :] % half, 0), axis=1)
    takes = new_holder[None, :] == (slots + side * half)[:, None]
    giver = jnp.sum(jnp.where(takes, labels[None, :], 0), axis=1)
    rank_of = jnp.sum(jnp.where(takes, rank[None, :], 0), axis=1)
    local = (giver // half) == side
    count = jnp.sum(crosses) // 2
    return send, local, giver % half, rank_of, count


def pick_items(value, index):
    return jnp.stack([lax.dynamic_index_in_dim(value, index[k], 0, keepdims=False) for k in range(index.shape[0])])


def cross_some(value, send, start, size):
    return swap(pick_items(value, send[start : start + size]), value.shape[0])


def cross_rest(value, send, count):
    half = value.shape[0]
    base = half // 2
    sizes = sorted({0, half // 8, half // 4, half // 2})

    def branch(extra):
        def run(held):
            if extra == 0:
                return jnp.zeros((half - base,) + held.shape[1:], held.dtype)
            came = cross_some(held, send, base, extra)
            if extra == half - base:
                return came
            rest = jnp.zeros((half - base - extra,) + held.shape[1:], held.dtype)
            return jnp.concatenate([came, rest])

        return run

    over = count - base
    which = sum((over > s).astype(jnp.int32) for s in sizes[:-1])
    return lax.switch(which, [branch(s) for s in sizes], value)


def chosen(table, i, held):
    value = held[0][0]
    for k in range(1, len(held)):
        value = jnp.where(table[0, i] == k, held[k][0], value)
    return value.astype(jnp.float32)


def first_body(table, *refs):
    *held, grad, out = refs
    old = chosen(table, pl.program_id(0), held)
    out[0] = (beta_first * old + (1.0 - beta_first) * grad[0]).astype(out.dtype)


def second_body(table, *refs):
    *held, grad, out = refs
    old = chosen(table, pl.program_id(0), held)
    g = grad[0]
    out[0] = (beta_second * old + (1.0 - beta_second) * g * g).astype(out.dtype)


def fresh_body(table, *refs):
    *held, first, second, out = refs
    master = chosen(table, pl.program_id(0), held)
    mean = first[0].astype(jnp.float32) / fix_first
    scale = jnp.sqrt(second[0].astype(jnp.float32) / fix_second) + adam_eps
    out[0] = (master - learn_rate * (mean / scale + decay_rate * master)).astype(out.dtype)


def per_item(body, table, held, extras):
    items, rows, columns = held[0].shape
    block = (1, rows, columns)

    def held_spec(k):
        return pl.BlockSpec(block, lambda i, t: (t[1 + k, i], 0, 0))

    specs = [held_spec(k) for k in range(len(held))]
    specs += [pl.BlockSpec(block, lambda i, t: (i, 0, 0)) for _ in extras]
    return pl.pallas_call(
        body,
        grid_spec=pltpu.PrefetchScalarGridSpec(
            num_scalar_prefetch=1,
            grid=(items,),
            in_specs=specs,
            out_specs=pl.BlockSpec(block, lambda i, t: (i, 0, 0)),
        ),
        out_shape=jax.ShapeDtypeStruct(held[0].shape, jnp.bfloat16),
        compiler_params=pltpu.CompilerParams(vmem_limit_bytes=32 * 1024 * 1024),
        cost_estimate=pl.CostEstimate(
            flops=10 * held[0].size, bytes_accessed=(6 + 4 * len(extras)) * held[0].size, transcendentals=0
        ),
    )(table, *held, *extras)


def per_device(
    tokens,
    route_weight,
    route_expert,
    cotangent,
    gate_quant,
    up_quant,
    gate_scale,
    up_scale,
    down_quant,
    down_scale,
    first_moment,
    second_moment,
    old_expert,
    new_holder,
):
    number = lax.axis_size("expert")
    dp_size = lax.axis_size("dp")
    me = lax.axis_index("expert")
    part = lax.axis_index("dp")
    half = number // 2
    tok_rows = tokens.shape[0]
    hidden_rows, columns = down_quant.shape[1:]
    unit_rows = hidden_rows // half
    item_shape = (half, unit_rows, columns)

    send, local, giver_slot, rank_of, count = routing(new_holder, me)
    base = half // 2
    one, two = base // 4, base // 2

    def table_of(sizes):
        starts = [sum(sizes[:k]) for k in range(len(sizes) + 1)]
        piece = sum((rank_of >= start).astype(jnp.int32) for start in starts)
        place = jnp.where(local, 0, piece)
        rows = [place, jnp.where(local, giver_slot, 0)]
        rows += [jnp.where(place == 1 + k, rank_of - start, 0) for k, start in enumerate(starts)]
        return jnp.stack(rows).astype(jnp.int32)

    share = tok_rows // dp_size
    blocks = jnp.arange(number, dtype=jnp.int32)
    labels = jnp.arange(number, dtype=jnp.int32)
    rows_of = tokens.reshape(dp_size, share, -1)
    token_own = [lax.dynamic_index_in_dim(rows_of, part, 0, keepdims=False)]
    for q in range(1, dp_size):
        token_own.append(swap_part(lax.dynamic_index_in_dim(rows_of, part ^ q, 0, keepdims=False), q))
    token_own = jnp.concatenate(in_order(token_own), axis=1)
    gates = all_parts(gate_quant[0])
    ups = all_parts(up_quant[0])
    gate_scales = all_parts(gate_scale[0])
    up_scales = all_parts(up_scale[0])
    first_moment = first_moment[0].astype(jnp.bfloat16).reshape(item_shape)
    token_lines = gather_lines(token_own)

    def own_rows(value):
        return lax.dynamic_slice_in_dim(value, part * share, share, 0)

    named = (own_rows(route_expert)[:, :, None] == labels).astype(jnp.float32)
    weight_own = jnp.sum(named * own_rows(route_weight)[:, :, None], axis=1)
    weight_lines = gather_lines(weight_own)
    back_lines = gather_lines(cotangent)
    first_out = half_exchange(first_moment)
    down_w = dequantize(down_quant[0], down_scale[0]).astype(jnp.bfloat16)
    token_lines, weight_lines, back_lines, first_out, down_w = fence(
        token_lines, weight_lines, back_lines, first_out, down_w
    )

    token_pair = gather_near(after(token_lines, gates[-1], ups[-1], gate_scales[-1], up_scales[-1]))
    weight_pair = gather_near(weight_lines)
    first_a = cross_some(first_out, send, 0, one)
    token_pair, weight_pair, first_a, first_out = fence(token_pair, weight_pair, first_a, first_out)

    whole = gather_far(token_pair)
    gates = [dequantize(quant, after(scale, token_pair)) for quant, scale in zip(gates, gate_scales)]
    ups = [dequantize(quant, after(scale, token_pair)) for quant, scale in zip(ups, up_scales)]
    gates = [gate.astype(jnp.bfloat16) for gate in gates]
    ups = [up.astype(jnp.bfloat16) for up in ups]
    second_moment = after(second_moment[0], token_pair).astype(jnp.bfloat16).reshape(item_shape)
    weight_all = gather_far(weight_pair)
    first_b = cross_some(first_out, send, one, one)
    whole, weight_all, first_b, first_out, second_moment = fence(
        whole, weight_all, first_b, first_out, second_moment
    )

    held_label = jnp.sum(jnp.where(labels == me, old_expert, 0))
    weight_rows = jnp.sum(jnp.where(labels == held_label, weight_all, 0.0), axis=1, keepdims=True)
    hidden = []
    for q in range(dp_size):
        gate_val = jnp.dot(whole, gates[q], preferred_element_type=jnp.float32)
        up_val = jnp.dot(whole, ups[q], preferred_element_type=jnp.float32)
        hidden.append((jax.nn.silu(gate_val) * up_val * weight_rows).astype(jnp.bfloat16))
    hidden = jnp.concatenate(in_order(hidden), axis=1)
    sent = jnp.take(hidden.reshape(number, share, hidden_rows), me ^ blocks, axis=0)
    sent = sent.reshape(number * share, half, unit_rows).transpose(1, 0, 2)
    second_out = half_exchange(second_moment)
    first_c = cross_some(first_out, send, 2 * one, one)
    hidden, sent, second_out, first_c, first_out, back_lines = fence(
        hidden, sent, second_out, first_c, first_out, back_lines
    )

    hid_own = half_exchange(sent)
    back_pair = gather_near(back_lines)
    first_d = cross_some(first_out, send, 3 * one, one)
    hid_own, back_pair, first_d, first_out, hidden, second_out = fence(
        hid_own, back_pair, first_d, first_out, hidden, second_out
    )

    hid_came = cross_some(hid_own, send, 0, base)
    hid_rest = cross_rest(hid_own, send, count)
    back = gather_far(back_pair)
    hidden_all = in_order(all_parts(hidden.reshape(number, share, hidden_rows)))
    hidden_all = jnp.stack(hidden_all, axis=1).reshape(number * tok_rows, hidden_rows)
    hid_came, hid_rest, back, hidden_all, second_out, down_w = fence(
        hid_came, hid_rest, back, hidden_all, second_out, down_w
    )

    down_out = half_exchange(down_w.reshape(item_shape))
    second_a = cross_some(second_out, send, 0, two)
    hid_items = jnp.where(
        local[:, None, None],
        jnp.take(hid_own, giver_slot, axis=0),
        jnp.take(jnp.concatenate([hid_came, hid_rest]), rank_of, axis=0),
    )
    out_part = jnp.dot(hidden_all, down_w, preferred_element_type=jnp.float32).astype(jnp.bfloat16)
    back = back.reshape(number, dp_size, share, columns)
    backs = [jnp.take(back[:, p], me ^ blocks, axis=0).reshape(-1, columns) for p in range(dp_size)]
    down_out, second_a, hid_items, out_part, second_out, *backs = fence(
        down_out, second_a, hid_items, out_part, second_out, *backs
    )

    hid_parts = in_order(all_parts(hid_items))
    kept, near = scatter_far(out_part.reshape(number, tok_rows, columns))
    second_b = cross_some(second_out, send, two, two)
    grad = lax.dot_general(
        jnp.concatenate(hid_parts, axis=1),
        jnp.concatenate(backs, axis=0),
        (((1,), (0,)), ((), ())),
        preferred_element_type=jnp.float32,
    )
    first_held = (first_out, first_a, first_b, first_c, first_d, cross_rest(first_out, send, count))
    first_new = per_item(first_body, table_of((one, one, one, one)), first_held, (grad,))
    kept, near, second_b, grad, first_new, down_out = fence(
        kept, near, second_b, grad, first_new, down_out
    )

    first_home = half_exchange(first_new)
    down_a = cross_some(down_out, send, 0, two)
    lines = scatter_near(kept, near)
    second_held = (second_out, second_a, second_b, cross_rest(second_out, send, count))
    second_new = per_item(second_body, table_of((two, two)), second_held, (grad,))
    first_home, down_a, lines, second_new, down_out = fence(
        first_home, down_a, lines, second_new, down_out
    )

    second_home = half_exchange(second_new)
    down_b = cross_some(down_out, send, two, two)
    mixed = scatter_lines(lines)
    first_full = first_home.astype(jnp.float32)
    second_home, down_b, first_full, mixed = fence(second_home, down_b, first_full, mixed)

    down_held = (down_out, down_a, down_b, cross_rest(down_out, send, count))
    fresh = per_item(fresh_body, table_of((two, two)), down_held, (first_new, second_new))
    fresh_home = half_exchange(fresh)
    second_full = second_home.astype(jnp.float32)

    home = (1, hidden_rows, columns)
    return (mixed, fresh_home.reshape(home), first_full.reshape(home), second_full.reshape(home))


def solution(mesh):
    in_specs = (
        P("expert", "dp"),
        P("expert", None),
        P("expert", None),
        P("expert", "dp"),
        P("expert", None, "dp"),
        P("expert", None, "dp"),
        P("expert", None, "dp"),
        P("expert", None, "dp"),
        P("expert", None, "dp"),
        P("expert", None, "dp"),
        P("expert", None, "dp"),
        P("expert", None, "dp"),
        P(),
        P(),
    )
    out_specs = (
        P("expert", "dp"),
        P("expert", None, "dp"),
        P("expert", None, "dp"),
        P("expert", None, "dp"),
    )
    return jax.shard_map(
        per_device, mesh=mesh, in_specs=in_specs, out_specs=out_specs, check_vma=False
    )
```

```python
import jax
import jax.numpy as jnp
from jax import lax
from jax.experimental import pallas as pl
from jax.experimental.pallas import tpu as pltpu
from jax.sharding import PartitionSpec as P

QB = 128
INNER = 4

beta_first = 0.9
beta_second = 0.95
adam_eps = 1e-08
learn_rate = 0.003
decay_rate = 0.1
step_count = 20
fix_first = 1.0 - beta_first**step_count
fix_second = 1.0 - beta_second**step_count


def dequantize(quant, scale):
    rows, columns = quant.shape
    across = jnp.repeat(scale, QB, axis=1)
    tiles = quant.astype(jnp.float32).reshape(rows // QB, QB, columns) * across[:, None, :]
    return tiles.reshape(rows, columns)


def swap(value, bits):
    number = lax.axis_size("expert")
    return lax.ppermute(value, "expert", [(i, i ^ bits) for i in range(number)])


def swap_part(value, bits):
    number = lax.axis_size("dp")
    return lax.ppermute(value, "dp", [(i, i ^ bits) for i in range(number)])


def in_order(held):
    part = lax.axis_index("dp")
    pieces = []
    for p in range(len(held)):
        piece = held[0]
        for q in range(1, len(held)):
            piece = jnp.where((part ^ p) == q, held[q], piece)
        pieces.append(piece)
    return pieces


def all_parts(value):
    return [value] + [swap_part(value, q) for q in range(1, lax.axis_size("dp"))]


def fence(*values):
    return lax.optimization_barrier(values)


def after(value, *earlier):
    zero = 0.0
    for array in earlier:
        zero = zero + array[(-1,) * array.ndim].astype(jnp.float32) * 0.0
    return value + zero.astype(value.dtype)


def swap_turn(value, step):
    number, parts = lax.axis_size("expert"), lax.axis_size("dp")
    pairs = []
    for i in range(number):
        for p in range(parts):
            bits = 1 if (p + step) % 2 == 0 else 2
            pairs.append((i * parts + p, (i ^ bits) * parts + p))
    return lax.ppermute(value, ("expert", "dp"), pairs)


def in_turn(even, odd):
    return jnp.where(lax.axis_index("dp") % 2 == 0, even, odd)


def gather_lines(block):
    outer = lax.axis_size("expert") // INNER
    return jnp.stack([block] + [swap(block, INNER * k) for k in range(1, outer)])


def gather_near(lines):
    return jnp.stack([lines, swap_turn(lines, 0)])


def gather_far(pair):
    far = swap_turn(pair, 1)
    full = jnp.stack([pair[0], in_turn(pair[1], far[0]), in_turn(far[0], pair[1]), far[1]], axis=1)
    return full.reshape((-1,) + pair.shape[3:])


def add(mine, other):
    return mine.astype(jnp.float32) + other.astype(jnp.float32)


def scatter_far(parts):
    number, rows, columns = parts.shape
    grid = parts.reshape(number // INNER, INNER, rows, columns)
    near, far = in_turn(grid[:, 1], grid[:, 2]), in_turn(grid[:, 2], grid[:, 1])
    came = swap_turn(jnp.stack([far, grid[:, 3]]), 1)
    return add(grid[:, 0], came[0]).astype(jnp.bfloat16), add(near, came[1]).astype(jnp.bfloat16)


def scatter_near(kept, near):
    return add(kept, swap_turn(near, 0)).astype(jnp.bfloat16)


def scatter_lines(lines):
    total = lines[0].astype(jnp.float32)
    for k in range(1, lines.shape[0]):
        total = total + swap(lines[k], INNER * k).astype(jnp.float32)
    return total.astype(jnp.bfloat16)


def half_exchange(value):
    number = lax.axis_size("expert")
    half = number // 2
    groups = [list(range(half)), list(range(half, number))]
    return lax.all_to_all(
        value, "expert", split_axis=0, concat_axis=0, tiled=True, axis_index_groups=groups
    )


def routing(new_holder, me):
    number = new_holder.shape[0]
    half = number // 2
    side = me // half
    labels = jnp.arange(number, dtype=jnp.int32)
    crosses = ((new_holder // half) != (labels // half)).astype(jnp.int32)
    same = (labels[:, None] // half) == (labels[None, :] // half)
    earlier = same & (labels[None, :] < labels[:, None])
    rank = jnp.sum(jnp.where(earlier, crosses[None, :], 0), axis=1)
    slots = jnp.arange(half, dtype=jnp.int32)
    mine = (labels // half) == side
    leaves = (rank[None, :] == slots[:, None]) & (crosses[None, :] > 0) & mine[None, :]
    send = jnp.sum(jnp.where(leaves, labels[None, :] % half, 0), axis=1)
    takes = new_holder[None, :] == (slots + side * half)[:, None]
    giver = jnp.sum(jnp.where(takes, labels[None, :], 0), axis=1)
    rank_of = jnp.sum(jnp.where(takes, rank[None, :], 0), axis=1)
    local = (giver // half) == side
    count = jnp.sum(crosses) // 2
    return send, local, giver % half, rank_of, count


def pick_items(value, index):
    return jnp.stack([lax.dynamic_index_in_dim(value, index[k], 0, keepdims=False) for k in range(index.shape[0])])


def cross_some(value, send, start, size):
    return swap(pick_items(value, send[start : start + size]), value.shape[0])


def cross_rest(value, send, count):
    half = value.shape[0]
    base = half // 2
    sizes = sorted({0, half // 8, half // 4, half // 2})

    def branch(extra):
        def run(held):
            if extra == 0:
                return jnp.zeros((half - base,) + held.shape[1:], held.dtype)
            came = cross_some(held, send, base, extra)
            if extra == half - base:
                return came
            rest = jnp.zeros((half - base - extra,) + held.shape[1:], held.dtype)
            return jnp.concatenate([came, rest])

        return run

    over = count - base
    which = sum((over > s).astype(jnp.int32) for s in sizes[:-1])
    return lax.switch(which, [branch(s) for s in sizes], value)


def chosen(table, i, held):
    value = held[0][0]
    for k in range(1, len(held)):
        value = jnp.where(table[0, i] == k, held[k][0], value)
    return value.astype(jnp.float32)


def first_body(table, *refs):
    *held, grad, out = refs
    old = chosen(table, pl.program_id(0), held)
    out[0] = (beta_first * old + (1.0 - beta_first) * grad[0]).astype(out.dtype)


def second_body(table, *refs):
    *held, grad, out = refs
    old = chosen(table, pl.program_id(0), held)
    g = grad[0]
    out[0] = (beta_second * old + (1.0 - beta_second) * g * g).astype(out.dtype)


def fresh_body(table, *refs):
    *held, first, second, out = refs
    master = chosen(table, pl.program_id(0), held)
    mean = first[0].astype(jnp.float32) / fix_first
    scale = jnp.sqrt(second[0].astype(jnp.float32) / fix_second) + adam_eps
    out[0] = (master - learn_rate * (mean / scale + decay_rate * master)).astype(out.dtype)


def per_item(body, table, held, extras):
    items, rows, columns = held[0].shape
    block = (1, rows, columns)

    def held_spec(k):
        return pl.BlockSpec(block, lambda i, t: (t[1 + k, i], 0, 0))

    specs = [held_spec(k) for k in range(len(held))]
    specs += [pl.BlockSpec(block, lambda i, t: (i, 0, 0)) for _ in extras]
    return pl.pallas_call(
        body,
        grid_spec=pltpu.PrefetchScalarGridSpec(
            num_scalar_prefetch=1,
            grid=(items,),
            in_specs=specs,
            out_specs=pl.BlockSpec(block, lambda i, t: (i, 0, 0)),
        ),
        out_shape=jax.ShapeDtypeStruct(held[0].shape, jnp.bfloat16),
        compiler_params=pltpu.CompilerParams(vmem_limit_bytes=32 * 1024 * 1024),
        cost_estimate=pl.CostEstimate(
            flops=10 * held[0].size, bytes_accessed=(6 + 4 * len(extras)) * held[0].size, transcendentals=0
        ),
    )(table, *held, *extras)


def per_device(
    tokens,
    route_weight,
    route_expert,
    cotangent,
    gate_quant,
    up_quant,
    gate_scale,
    up_scale,
    down_quant,
    down_scale,
    first_moment,
    second_moment,
    old_expert,
    new_holder,
):
    number = lax.axis_size("expert")
    dp_size = lax.axis_size("dp")
    me = lax.axis_index("expert")
    part = lax.axis_index("dp")
    half = number // 2
    tok_rows = tokens.shape[0]
    hidden_rows, columns = down_quant.shape[1:]
    unit_rows = hidden_rows // half
    item_shape = (half, unit_rows, columns)

    send, local, giver_slot, rank_of, count = routing(new_holder, me)
    base = half // 2
    one, two = base // 4, base // 2

    def table_of(sizes):
        starts = [sum(sizes[:k]) for k in range(len(sizes) + 1)]
        piece = sum((rank_of >= start).astype(jnp.int32) for start in starts)
        place = jnp.where(local, 0, piece)
        rows = [place, jnp.where(local, giver_slot, 0)]
        rows += [jnp.where(place == 1 + k, rank_of - start, 0) for k, start in enumerate(starts)]
        return jnp.stack(rows).astype(jnp.int32)

    share = tok_rows // dp_size
    blocks = jnp.arange(number, dtype=jnp.int32)
    labels = jnp.arange(number, dtype=jnp.int32)
    rows_of = tokens.reshape(dp_size, share, -1)
    token_own = [lax.dynamic_index_in_dim(rows_of, part, 0, keepdims=False)]
    for q in range(1, dp_size):
        token_own.append(swap_part(lax.dynamic_index_in_dim(rows_of, part ^ q, 0, keepdims=False), q))
    token_own = jnp.concatenate(in_order(token_own), axis=1)
    columns_of = list(zip(all_parts(gate_quant[0]), all_parts(gate_scale[0])))
    columns_of += list(zip(all_parts(up_quant[0]), all_parts(up_scale[0])))
    gate_up = jnp.concatenate(
        [dequantize(quant, scale).astype(jnp.bfloat16) for quant, scale in columns_of], axis=1
    )
    token_lines = gather_lines(token_own)

    def own_rows(value):
        return lax.dynamic_slice_in_dim(value, part * share, share, 0)

    named = (own_rows(route_expert)[:, :, None] == labels).astype(jnp.float32)
    weight_own = jnp.sum(named * own_rows(route_weight)[:, :, None], axis=1)
    weight_all = gather_far(gather_near(gather_lines(weight_own)))
    held_label = jnp.sum(jnp.where(labels == me, old_expert, 0))
    weight_rows = jnp.sum(jnp.where(labels == held_label, weight_all, 0.0), axis=1, keepdims=True)
    back_lines = gather_lines(cotangent)
    whole = gather_far(gather_near(after(token_lines, gate_up, weight_rows)))

    first_moment = after(first_moment[0], whole, back_lines).astype(jnp.bfloat16)
    first_out = half_exchange(first_moment.reshape(item_shape))
    down_w = dequantize(down_quant[0], down_scale[0]).astype(jnp.bfloat16)
    value = jnp.dot(whole, gate_up, preferred_element_type=jnp.float32)
    units = gate_quant.shape[2]
    hidden = []
    for q in range(dp_size):
        gate_val = value[:, q * units : (q + 1) * units]
        up_val = value[:, hidden_rows + q * units : hidden_rows + (q + 1) * units]
        hidden.append((jax.nn.silu(gate_val) * up_val * weight_rows).astype(jnp.bfloat16))
    hidden = jnp.concatenate(in_order(hidden), axis=1)
    sent = jnp.take(hidden.reshape(number, share, hidden_rows), me ^ blocks, axis=0)
    sent = sent.reshape(number * share, half, unit_rows).transpose(1, 0, 2)
    hidden, sent, first_out, back_lines, down_w = fence(hidden, sent, first_out, back_lines, down_w)

    hid_own = half_exchange(after(sent, first_out))
    back_pair = gather_near(back_lines)
    first_a = cross_some(first_out, send, 0, one)
    hid_own, back_pair, first_a, first_out, hidden = fence(
        hid_own, back_pair, first_a, first_out, hidden
    )

    hid_came = cross_some(hid_own, send, 0, base)
    hid_rest = cross_rest(hid_own, send, count)
    back = gather_far(back_pair)
    first_b = cross_some(first_out, send, one, one)
    hidden_all = in_order(all_parts(hidden.reshape(number, share, hidden_rows)))
    hidden_all = jnp.stack(hidden_all, axis=1).reshape(number * tok_rows, hidden_rows)
    second_moment = after(second_moment[0], hid_own).astype(jnp.bfloat16).reshape(item_shape)
    hid_came, hid_rest, back, first_b, first_out, hidden_all, second_moment, down_w = fence(
        hid_came, hid_rest, back, first_b, first_out, hidden_all, second_moment, down_w
    )

    second_out = half_exchange(second_moment)
    first_c = cross_some(first_out, send, two, two)
    hid_items = jnp.where(
        local[:, None, None],
        jnp.take(hid_own, giver_slot, axis=0),
        jnp.take(jnp.concatenate([hid_came, hid_rest]), rank_of, axis=0),
    )
    back = back.reshape(number, dp_size, share, columns)
    backs = [jnp.take(back[:, p], me ^ blocks, axis=0).reshape(-1, columns) for p in range(dp_size)]
    second_out, first_c, hid_items, hidden_all, down_w, *backs = fence(
        second_out, first_c, hid_items, hidden_all, down_w, *backs
    )

    down_out = half_exchange(after(down_w, second_out).reshape(item_shape))
    second_a = cross_some(second_out, send, 0, two)
    out_part = jnp.dot(hidden_all, down_w, preferred_element_type=jnp.float32).astype(jnp.bfloat16)
    down_out, second_a, out_part, second_out, hid_items = fence(
        down_out, second_a, out_part, second_out, hid_items
    )

    hid_parts = in_order(all_parts(hid_items))
    kept, near = scatter_far(out_part.reshape(number, tok_rows, columns))
    second_b = cross_some(second_out, send, two, two)
    grad = lax.dot_general(
        jnp.concatenate(hid_parts, axis=1),
        jnp.concatenate(backs, axis=0),
        (((1,), (0,)), ((), ())),
        preferred_element_type=jnp.float32,
    )
    first_held = (first_out, first_a, first_b, first_c, cross_rest(first_out, send, count))
    first_new = per_item(first_body, table_of((one, one, two)), first_held, (grad,))
    kept, near, second_b, grad, first_new, down_out = fence(
        kept, near, second_b, grad, first_new, down_out
    )

    first_home = half_exchange(first_new)
    down_a = cross_some(down_out, send, 0, two)
    lines = scatter_near(kept, near)
    second_held = (second_out, second_a, second_b, cross_rest(second_out, send, count))
    second_new = per_item(second_body, table_of((two, two)), second_held, (grad,))
    first_home, down_a, lines, second_new, down_out = fence(
        first_home, down_a, lines, second_new, down_out
    )

    second_home = half_exchange(second_new)
    down_b = cross_some(down_out, send, two, two)
    mixed = scatter_lines(lines)
    first_full = first_home.astype(jnp.float32)
    second_home, down_b, first_full, mixed = fence(second_home, down_b, first_full, mixed)

    down_held = (down_out, down_a, down_b, cross_rest(down_out, send, count))
    fresh = per_item(fresh_body, table_of((two, two)), down_held, (first_new, second_new))
    fresh_home = half_exchange(fresh)
    second_full = second_home.astype(jnp.float32)

    home = (1, hidden_rows, columns)
    return (mixed, fresh_home.reshape(home), first_full.reshape(home), second_full.reshape(home))


def solution(mesh):
    in_specs = (
        P("expert", "dp"),
        P("expert", None),
        P("expert", None),
        P("expert", "dp"),
        P("expert", None, "dp"),
        P("expert", None, "dp"),
        P("expert", None, "dp"),
        P("expert", None, "dp"),
        P("expert", None, "dp"),
        P("expert", None, "dp"),
        P("expert", None, "dp"),
        P("expert", None, "dp"),
        P(),
        P(),
    )
    out_specs = (
        P("expert", "dp"),
        P("expert", None, "dp"),
        P("expert", None, "dp"),
        P("expert", None, "dp"),
    )
    return jax.shard_map(
        per_device, mesh=mesh, in_specs=in_specs, out_specs=out_specs, check_vma=False
    )
```

```python
import jax
import jax.numpy as jnp
from jax import lax
from jax.experimental import pallas as pl
from jax.experimental.pallas import tpu as pltpu
from jax.sharding import PartitionSpec as P

QB = 128
INNER = 4

beta_first = 0.9
beta_second = 0.95
adam_eps = 1e-08
learn_rate = 0.003
decay_rate = 0.1
step_count = 20
fix_first = 1.0 - beta_first**step_count
fix_second = 1.0 - beta_second**step_count


def dequantize(quant, scale):
    rows, columns = quant.shape
    across = jnp.repeat(scale, QB, axis=1)
    tiles = quant.astype(jnp.float32).reshape(rows // QB, QB, columns) * across[:, None, :]
    return tiles.reshape(rows, columns)


def swap(value, bits):
    number = lax.axis_size("expert")
    return lax.ppermute(value, "expert", [(i, i ^ bits) for i in range(number)])


def swap_part(value, bits):
    number = lax.axis_size("dp")
    return lax.ppermute(value, "dp", [(i, i ^ bits) for i in range(number)])


def in_order(held):
    part = lax.axis_index("dp")
    pieces = []
    for p in range(len(held)):
        piece = held[0]
        for q in range(1, len(held)):
            piece = jnp.where((part ^ p) == q, held[q], piece)
        pieces.append(piece)
    return pieces


def all_parts(value):
    return [value] + [swap_part(value, q) for q in range(1, lax.axis_size("dp"))]


def fence(*values):
    return lax.optimization_barrier(values)


def after(value, *earlier):
    zero = 0.0
    for array in earlier:
        zero = zero + array[(-1,) * array.ndim].astype(jnp.float32) * 0.0
    return value + zero.astype(value.dtype)


def swap_turn(value, step):
    number, parts = lax.axis_size("expert"), lax.axis_size("dp")
    pairs = []
    for i in range(number):
        for p in range(parts):
            bits = 1 if (p + step) % 2 == 0 else 2
            pairs.append((i * parts + p, (i ^ bits) * parts + p))
    return lax.ppermute(value, ("expert", "dp"), pairs)


def in_turn(even, odd):
    return jnp.where(lax.axis_index("dp") % 2 == 0, even, odd)


def gather_lines(block):
    outer = lax.axis_size("expert") // INNER
    return jnp.stack([block] + [swap(block, INNER * k) for k in range(1, outer)])


def gather_near(lines):
    return jnp.stack([lines, swap_turn(lines, 0)])


def gather_far(pair):
    far = swap_turn(pair, 1)
    full = jnp.stack([pair[0], in_turn(pair[1], far[0]), in_turn(far[0], pair[1]), far[1]], axis=1)
    return full.reshape((-1,) + pair.shape[3:])


def add(mine, other):
    return mine.astype(jnp.float32) + other.astype(jnp.float32)


def scatter_far(parts):
    number, rows, columns = parts.shape
    grid = parts.reshape(number // INNER, INNER, rows, columns)
    near, far = in_turn(grid[:, 1], grid[:, 2]), in_turn(grid[:, 2], grid[:, 1])
    came = swap_turn(jnp.stack([far, grid[:, 3]]), 1)
    return add(grid[:, 0], came[0]).astype(jnp.bfloat16), add(near, came[1]).astype(jnp.bfloat16)


def scatter_near(kept, near):
    return add(kept, swap_turn(near, 0)).astype(jnp.bfloat16)


def scatter_lines(lines):
    total = lines[0].astype(jnp.float32)
    for k in range(1, lines.shape[0]):
        total = total + swap(lines[k], INNER * k).astype(jnp.float32)
    return total.astype(jnp.bfloat16)


def half_exchange(value):
    number = lax.axis_size("expert")
    half = number // 2
    groups = [list(range(half)), list(range(half, number))]
    return lax.all_to_all(
        value, "expert", split_axis=0, concat_axis=0, tiled=True, axis_index_groups=groups
    )


def routing(new_holder, me):
    number = new_holder.shape[0]
    half = number // 2
    side = me // half
    labels = jnp.arange(number, dtype=jnp.int32)
    crosses = ((new_holder // half) != (labels // half)).astype(jnp.int32)
    same = (labels[:, None] // half) == (labels[None, :] // half)
    earlier = same & (labels[None, :] < labels[:, None])
    rank = jnp.sum(jnp.where(earlier, crosses[None, :], 0), axis=1)
    slots = jnp.arange(half, dtype=jnp.int32)
    mine = (labels // half) == side
    leaves = (rank[None, :] == slots[:, None]) & (crosses[None, :] > 0) & mine[None, :]
    send = jnp.sum(jnp.where(leaves, labels[None, :] % half, 0), axis=1)
    takes = new_holder[None, :] == (slots + side * half)[:, None]
    giver = jnp.sum(jnp.where(takes, labels[None, :], 0), axis=1)
    rank_of = jnp.sum(jnp.where(takes, rank[None, :], 0), axis=1)
    local = (giver // half) == side
    count = jnp.sum(crosses) // 2
    return send, local, giver % half, rank_of, count


def pick_items(value, index):
    return jnp.stack([lax.dynamic_index_in_dim(value, index[k], 0, keepdims=False) for k in range(index.shape[0])])


def cross_some(value, send, start, size):
    return swap(pick_items(value, send[start : start + size]), value.shape[0])


def cross_rest(value, send, count):
    half = value.shape[0]
    base = half // 2
    sizes = sorted({0, half // 8, half // 4, half // 2})

    def branch(extra):
        def run(held):
            if extra == 0:
                return jnp.zeros((half - base,) + held.shape[1:], held.dtype)
            came = cross_some(held, send, base, extra)
            if extra == half - base:
                return came
            rest = jnp.zeros((half - base - extra,) + held.shape[1:], held.dtype)
            return jnp.concatenate([came, rest])

        return run

    over = count - base
    which = sum((over > s).astype(jnp.int32) for s in sizes[:-1])
    return lax.switch(which, [branch(s) for s in sizes], value)


def chosen(table, i, held):
    value = held[0][0]
    for k in range(1, len(held)):
        value = jnp.where(table[0, i] == k, held[k][0], value)
    return value.astype(jnp.float32)


def first_body(table, *refs):
    *held, grad, out = refs
    old = chosen(table, pl.program_id(0), held)
    out[0] = (beta_first * old + (1.0 - beta_first) * grad[0]).astype(out.dtype)


def second_body(table, *refs):
    *held, grad, out = refs
    old = chosen(table, pl.program_id(0), held)
    g = grad[0]
    out[0] = (beta_second * old + (1.0 - beta_second) * g * g).astype(out.dtype)


def fresh_body(table, *refs):
    *held, first, second, out = refs
    master = chosen(table, pl.program_id(0), held)
    mean = first[0].astype(jnp.float32) / fix_first
    scale = jnp.sqrt(second[0].astype(jnp.float32) / fix_second) + adam_eps
    out[0] = (master - learn_rate * (mean / scale + decay_rate * master)).astype(out.dtype)


def per_item(body, table, held, extras):
    items, rows, columns = held[0].shape
    block = (1, rows, columns)

    def held_spec(k):
        return pl.BlockSpec(block, lambda i, t: (t[1 + k, i], 0, 0))

    specs = [held_spec(k) for k in range(len(held))]
    specs += [pl.BlockSpec(block, lambda i, t: (i, 0, 0)) for _ in extras]
    return pl.pallas_call(
        body,
        grid_spec=pltpu.PrefetchScalarGridSpec(
            num_scalar_prefetch=1,
            grid=(items,),
            in_specs=specs,
            out_specs=pl.BlockSpec(block, lambda i, t: (i, 0, 0)),
        ),
        out_shape=jax.ShapeDtypeStruct(held[0].shape, jnp.bfloat16),
        compiler_params=pltpu.CompilerParams(vmem_limit_bytes=32 * 1024 * 1024),
        cost_estimate=pl.CostEstimate(
            flops=10 * held[0].size, bytes_accessed=(6 + 4 * len(extras)) * held[0].size, transcendentals=0
        ),
    )(table, *held, *extras)


def per_device(
    tokens,
    route_weight,
    route_expert,
    cotangent,
    gate_quant,
    up_quant,
    gate_scale,
    up_scale,
    down_quant,
    down_scale,
    first_moment,
    second_moment,
    old_expert,
    new_holder,
):
    number = lax.axis_size("expert")
    dp_size = lax.axis_size("dp")
    me = lax.axis_index("expert")
    part = lax.axis_index("dp")
    half = number // 2
    tok_rows = tokens.shape[0]
    hidden_rows, columns = down_quant.shape[1:]
    unit_rows = hidden_rows // half
    item_shape = (half, unit_rows, columns)

    send, local, giver_slot, rank_of, count = routing(new_holder, me)
    base = half // 2
    one, two = base // 4, base // 2

    def table_of(sizes):
        starts = [sum(sizes[:k]) for k in range(len(sizes) + 1)]
        piece = sum((rank_of >= start).astype(jnp.int32) for start in starts)
        place = jnp.where(local, 0, piece)
        rows = [place, jnp.where(local, giver_slot, 0)]
        rows += [jnp.where(place == 1 + k, rank_of - start, 0) for k, start in enumerate(starts)]
        return jnp.stack(rows).astype(jnp.int32)

    share = tok_rows // dp_size
    blocks = jnp.arange(number, dtype=jnp.int32)
    labels = jnp.arange(number, dtype=jnp.int32)
    rows_of = tokens.reshape(dp_size, share, -1)
    token_own = [lax.dynamic_index_in_dim(rows_of, part, 0, keepdims=False)]
    for q in range(1, dp_size):
        token_own.append(swap_part(lax.dynamic_index_in_dim(rows_of, part ^ q, 0, keepdims=False), q))
    token_own = jnp.concatenate(in_order(token_own), axis=1)
    gates = all_parts(gate_quant[0])
    ups = all_parts(up_quant[0])
    gate_scales = all_parts(gate_scale[0])
    up_scales = all_parts(up_scale[0])
    first_moment = first_moment[0].astype(jnp.bfloat16).reshape(item_shape)
    token_lines = gather_lines(token_own)

    def own_rows(value):
        return lax.dynamic_slice_in_dim(value, part * share, share, 0)

    named = (own_rows(route_expert)[:, :, None] == labels).astype(jnp.float32)
    weight_own = jnp.sum(named * own_rows(route_weight)[:, :, None], axis=1)
    weight_lines = gather_lines(weight_own)
    back_lines = gather_lines(cotangent)
    first_out = half_exchange(first_moment)
    down_w = dequantize(down_quant[0], down_scale[0]).astype(jnp.bfloat16)
    token_lines, weight_lines, back_lines, first_out, down_w = fence(
        token_lines, weight_lines, back_lines, first_out, down_w
    )

    gates = [dequantize(quant, scale) for quant, scale in zip(gates, gate_scales)]
    ups = [dequantize(quant, scale) for quant, scale in zip(ups, up_scales)]
    gates = [gate.astype(jnp.bfloat16) for gate in gates]
    ups = [up.astype(jnp.bfloat16) for up in ups]
    token_pair = gather_near(after(token_lines, *gates, *ups))
    weight_pair = gather_near(weight_lines)
    first_a = cross_some(first_out, send, 0, one)
    token_pair, weight_pair, first_a, first_out = fence(token_pair, weight_pair, first_a, first_out)

    whole = gather_far(token_pair)
    second_moment = after(second_moment[0], token_pair).astype(jnp.bfloat16).reshape(item_shape)
    weight_all = gather_far(weight_pair)
    first_b = cross_some(first_out, send, one, one)
    whole, weight_all, first_b, first_out, second_moment = fence(
        whole, weight_all, first_b, first_out, second_moment
    )

    held_label = jnp.sum(jnp.where(labels == me, old_expert, 0))
    weight_rows = jnp.sum(jnp.where(labels == held_label, weight_all, 0.0), axis=1, keepdims=True)
    hidden = []
    for q in range(dp_size):
        gate_val = jnp.dot(whole, gates[q], preferred_element_type=jnp.float32)
        up_val = jnp.dot(whole, ups[q], preferred_element_type=jnp.float32)
        hidden.append((jax.nn.silu(gate_val) * up_val * weight_rows).astype(jnp.bfloat16))
    hidden = jnp.concatenate(in_order(hidden), axis=1)
    sent = jnp.take(hidden.reshape(number, share, hidden_rows), me ^ blocks, axis=0)
    sent = sent.reshape(number * share, half, unit_rows).transpose(1, 0, 2)
    second_out = half_exchange(second_moment)
    first_c = cross_some(first_out, send, 2 * one, one)
    hidden, sent, second_out, first_c, first_out, back_lines = fence(
        hidden, sent, second_out, first_c, first_out, back_lines
    )

    hid_own = half_exchange(sent)
    back_pair = gather_near(back_lines)
    first_d = cross_some(first_out, send, 3 * one, one)
    hid_own, back_pair, first_d, first_out, hidden, second_out = fence(
        hid_own, back_pair, first_d, first_out, hidden, second_out
    )

    hid_came = cross_some(hid_own, send, 0, base)
    hid_rest = cross_rest(hid_own, send, count)
    back = gather_far(back_pair)
    hidden_all = in_order(all_parts(hidden.reshape(number, share, hidden_rows)))
    hidden_all = jnp.stack(hidden_all, axis=1).reshape(number * tok_rows, hidden_rows)
    hid_came, hid_rest, back, hidden_all, second_out, down_w = fence(
        hid_came, hid_rest, back, hidden_all, second_out, down_w
    )

    down_out = half_exchange(down_w.reshape(item_shape))
    second_a = cross_some(second_out, send, 0, two)
    hid_items = jnp.where(
        local[:, None, None],
        jnp.take(hid_own, giver_slot, axis=0),
        jnp.take(jnp.concatenate([hid_came, hid_rest]), rank_of, axis=0),
    )
    out_part = jnp.dot(hidden_all, down_w, preferred_element_type=jnp.float32).astype(jnp.bfloat16)
    back = back.reshape(number, dp_size, share, columns)
    backs = [jnp.take(back[:, p], me ^ blocks, axis=0).reshape(-1, columns) for p in range(dp_size)]
    down_out, second_a, hid_items, out_part, second_out, *backs = fence(
        down_out, second_a, hid_items, out_part, second_out, *backs
    )

    hid_parts = in_order(all_parts(hid_items))
    kept, near = scatter_far(out_part.reshape(number, tok_rows, columns))
    second_b = cross_some(second_out, send, two, two)
    grad = lax.dot_general(
        jnp.concatenate(hid_parts, axis=1),
        jnp.concatenate(backs, axis=0),
        (((1,), (0,)), ((), ())),
        preferred_element_type=jnp.float32,
    )
    first_held = (first_out, first_a, first_b, first_c, first_d, cross_rest(first_out, send, count))
    first_new = per_item(first_body, table_of((one, one, one, one)), first_held, (grad,))
    kept, near, second_b, grad, first_new, down_out = fence(
        kept, near, second_b, grad, first_new, down_out
    )

    first_home = half_exchange(first_new)
    down_a = cross_some(down_out, send, 0, two)
    lines = scatter_near(kept, near)
    second_held = (second_out, second_a, second_b, cross_rest(second_out, send, count))
    second_new = per_item(second_body, table_of((two, two)), second_held, (grad,))
    first_home, down_a, lines, second_new, down_out = fence(
        first_home, down_a, lines, second_new, down_out
    )

    second_home = half_exchange(second_new)
    down_b = cross_some(down_out, send, two, two)
    mixed = scatter_lines(lines)
    first_full = first_home.astype(jnp.float32)
    second_home, down_b, first_full, mixed = fence(second_home, down_b, first_full, mixed)

    down_held = (down_out, down_a, down_b, cross_rest(down_out, send, count))
    fresh = per_item(fresh_body, table_of((two, two)), down_held, (first_new, second_new))
    fresh_home = half_exchange(fresh)
    second_full = second_home.astype(jnp.float32)

    home = (1, hidden_rows, columns)
    return (mixed, fresh_home.reshape(home), first_full.reshape(home), second_full.reshape(home))


def solution(mesh):
    in_specs = (
        P("expert", "dp"),
        P("expert", None),
        P("expert", None),
        P("expert", "dp"),
        P("expert", None, "dp"),
        P("expert", None, "dp"),
        P("expert", None, "dp"),
        P("expert", None, "dp"),
        P("expert", None, "dp"),
        P("expert", None, "dp"),
        P("expert", None, "dp"),
        P("expert", None, "dp"),
        P(),
        P(),
    )
    out_specs = (
        P("expert", "dp"),
        P("expert", None, "dp"),
        P("expert", None, "dp"),
        P("expert", None, "dp"),
    )
    return jax.shard_map(
        per_device, mesh=mesh, in_specs=in_specs, out_specs=out_specs, check_vma=False
    )
```
